256 devices in a mesh: dp: 4 (over x_hi, core), ctx: 64 (over x_lo, y, z).
Axes of the slice: x: 4 (x_hi: 2, x_lo: 2; x = x_hi * 2 + x_lo), y: 4, z: 8, core: 2. Of those that a mesh axis runs over, the one named last changes fastest.
Arguments:
- tokens: int32 [4, 131072], P('dp', 'ctx'), may hold values from 0 to 255
- targets: int32 [4, 131072], P('dp', 'ctx'), may hold values from 0 to 255
- embed: bfloat16 [256, 256], replicated, may hold values from -6 to 6
- first_norm_gain: float32 [256], replicated, may hold values from 0.5 to 1.5
- first_kernel_weights: bfloat16 [3, 256, 512], replicated, may hold values from -0.21875 to 0.21875
- first_output_projection: bfloat16 [512, 256], replicated, may hold values from -0.25 to 0.25
- second_norm_gain: float32 [256], replicated, may hold values from 0.5 to 1.5
- second_kernel_weights: bfloat16 [3, 256, 512], replicated, may hold values from -0.21875 to 0.21875
- second_output_projection: bfloat16 [512, 256], replicated, may hold values from -0.25 to 0.25
- gain_final: float32 [256], replicated, may hold values from 0.5 to 1.5
- head: bfloat16 [256, 256], replicated, may hold values from -16 to 16
Outputs:
- token_loss: float32 [4, 131072], P('dp', 'ctx')
- grad_embed: float32 [256, 256], replicated
- first_norm_gain_gradient: float32 [256], replicated
- first_kernel_gradient: float32 [3, 256, 512], replicated
- first_projection_gradient: float32 [512, 256], replicated
- second_norm_gain_gradient: float32 [256], replicated
- second_kernel_gradient: float32 [3, 256, 512], replicated
- second_projection_gradient: float32 [512, 256], replicated
- grad_gain_final: float32 [256], replicated
- grad_head: float32 [256, 256], replicated
The draws below stay inside these ranges and needn't reach their ends.
All inputs are finite; a program needn't handle non-finite values.
Results may differ from the reference program's by a relative error of at most 0.0037.
Values may be sent and summed in bfloat16 or wider, within the bound.
No kernel may reach another device: no remote copies, remote signals or barrier semaphores. Data moves between devices by JAX's collectives and lax.ppermute only.
A program may use at most 64 MiB of HBM per device.

```python
import math
import jax
import jax.numpy as jnp
import numpy as np
from jax import lax

D = 256
HID = 512
VOCAB = 256
DOCS = 4
LENGTH = 131072
FIRST_DILATION = 2048
SECOND_DILATION = 4096


def draw_head(key, part):
    key = jax.random.fold_in(key, 7)
    spread = D ** (-0.5)
    base = jnp.clip(jax.random.normal(key, (D, VOCAB), jnp.float32), -6.0, 6.0) * spread
    return base.astype(jnp.bfloat16)


def touch_ends(entries, own_key, least, largest):
    longest = entries.shape.index(max(entries.shape))
    spots = []
    for shift in (0, 1):
        where = [jax.random.randint(jax.random.fold_in(own_key, axis), (), 0, length) for axis, length in enumerate(entries.shape)]
        where[longest] = (where[longest] + shift) % entries.shape[longest]
        spots.append(tuple(where))
    return entries.at[spots[0]].set(least).at[spots[1]].set(largest)


def cumulative_ranks(count, slope):
    weights = [(1 << 20) // math.isqrt(standing ** slope) + 1 for standing in range(1, count + 1)]
    scale = 1 + sum(weights) // (1 << 30)
    return np.cumsum(np.array([max(1, weight // scale) for weight in weights]))


def ranked(rng, extent, amount, slope):
    grid = cumulative_ranks(amount, slope)
    pick = jax.random.randint(jax.random.fold_in(rng, 1), extent, 0, int(grid[amount - 1]))
    grade = jnp.searchsorted(jnp.asarray(grid, jnp.int32), pick, side="right")
    return jax.random.permutation(jax.random.fold_in(rng, 2), amount)[grade].astype(jnp.int32)


def centred(key, extent, scale, reach, kind=jnp.bfloat16):
    return jnp.clip(scale * jax.random.normal(key, extent, jnp.float32), -reach, reach).astype(kind)


def setup_inputs(seed: int = 0) -> dict:
    keys = jax.random.split(jax.random.key(seed), 12)
    tokens = touch_ends(ranked(keys[0], (DOCS, LENGTH), VOCAB, 2), jax.random.fold_in(keys[0], 3), 0, VOCAB - 1).astype(jnp.int32)
    targets = touch_ends(ranked(keys[1], (DOCS, LENGTH), VOCAB, 1), jax.random.fold_in(keys[1], 3), 0, VOCAB - 1).astype(jnp.int32)
    embed = centred(keys[2], (VOCAB, D), 1.0, 6.0)
    first_norm_gain = jnp.clip(1.0 + 0.1 * jax.random.normal(keys[3], (D,), jnp.float32), 0.5, 1.5)
    first_kernel_weights = centred(keys[4], (3, D, HID), (3 * D) ** -0.5, 0.21875)
    first_output_projection = centred(keys[5], (HID, D), HID ** -0.5, 0.25)
    second_norm_gain = jnp.clip(1.0 + 0.1 * jax.random.normal(keys[6], (D,), jnp.float32), 0.5, 1.5)
    second_kernel_weights = centred(keys[7], (3, D, HID), (3 * D) ** -0.5, 0.21875)
    second_output_projection = centred(keys[8], (HID, D), HID ** -0.5, 0.25)
    gain_final = jnp.clip(1.0 + 0.1 * jax.random.normal(keys[9], (D,), jnp.float32), 0.5, 1.5)
    head = draw_head(jax.random.fold_in(keys[11], 71), 0)
    return {"tokens": tokens, "targets": targets, "embed": embed, "first_norm_gain": first_norm_gain, "first_kernel_weights": first_kernel_weights, "first_output_projection": first_output_projection, "second_norm_gain": second_norm_gain, "second_kernel_weights": second_kernel_weights, "second_output_projection": second_output_projection, "gain_final": gain_final, "head": head}


EPS = 1e-05

def contract_rows(left, right):
    return lax.dot_general(left, right, (((0,), (0,)), ((), ())), preferred_element_type=jnp.float32)

def contract_cols(left, right):
    return lax.dot_general(left, right, (((1,), (1,)), ((), ())), preferred_element_type=jnp.float32)

def rms_scale(values):
    return lax.rsqrt(lax.optimization_barrier(jnp.mean(values * values, axis=-1, keepdims=True)) + EPS)

def rms_back(values, scale, gain, grad_out):
    weighted = grad_out * gain
    grad_in = scale * weighted - values * scale ** 3 * lax.optimization_barrier(jnp.mean(weighted * values, axis=-1, keepdims=True))
    grad_gain = lax.optimization_barrier(jnp.sum(grad_out * values * scale, axis=0))
    return (grad_in, grad_gain)

def delay(values, dist):
    filler = jnp.zeros((dist, values.shape[1]), values.dtype)
    return jnp.concatenate([filler, values[:values.shape[0] - dist]], axis=0)

def advance(values, dist):
    filler = jnp.zeros((dist, values.shape[1]), values.dtype)
    return jnp.concatenate([values[dist:], filler], axis=0)

def residual_block_forward(values, gain, taps, out_w, dist):
    scale = rms_scale(values)
    normed = values * scale * gain
    hidden = jnp.maximum(normed, 0.0).astype(jnp.bfloat16)
    stacked = jnp.concatenate([hidden, delay(hidden, dist), delay(hidden, 2 * dist)], axis=1)
    conv = jnp.dot(stacked, taps.reshape(-1, taps.shape[2]), preferred_element_type=jnp.float32)
    active = jnp.maximum(conv, 0.0).astype(jnp.bfloat16)
    result = values + jnp.dot(active, out_w, preferred_element_type=jnp.float32)
    return (result, (values, scale, normed, stacked, conv, active))

def residual_block_backward(grad_out, saved, gain, taps, out_w, dist):
    values, scale, normed, stacked, conv, active = saved
    width = values.shape[1]
    grad_low = grad_out.astype(jnp.bfloat16)
    grad_out_w = contract_rows(active, grad_low)
    grad_active = contract_cols(grad_low, out_w)
    grad_conv = jnp.where(conv > 0, grad_active, 0.0).astype(jnp.bfloat16)
    grad_taps = contract_rows(stacked, grad_conv).reshape(taps.shape)
    returns = contract_cols(grad_conv, taps.reshape(-1, taps.shape[2])).astype(jnp.bfloat16)
    grad_hidden = returns[:, :width].astype(jnp.float32)
    grad_hidden = grad_hidden + advance(returns[:, width:2 * width], dist).astype(jnp.float32)
    grad_hidden = grad_hidden + advance(returns[:, 2 * width:], 2 * dist).astype(jnp.float32)
    grad_normed = jnp.where(normed > 0, grad_hidden, 0.0)
    grad_in, grad_gain = rms_back(values, scale, gain, grad_normed)
    return (grad_out + grad_in, grad_gain, grad_taps, grad_out_w)

def one_document(weights, toks, targs, loss_scale):
    embed, first_norm_gain, first_kernel_weights, first_output_projection, second_norm_gain, second_kernel_weights, second_output_projection, gain_final, head = weights
    letters = jnp.arange(embed.shape[0], dtype=jnp.int32)
    onehot = (toks[:, None] == letters[None, :]).astype(jnp.bfloat16)
    initial_activation = jnp.dot(onehot, embed, preferred_element_type=jnp.float32)
    between_blocks_activation, first_block_residuals = residual_block_forward(initial_activation, first_norm_gain, first_kernel_weights, first_output_projection, FIRST_DILATION)
    final_activation, second_block_residuals = residual_block_forward(between_blocks_activation, second_norm_gain, second_kernel_weights, second_output_projection, SECOND_DILATION)
    final_scale = rms_scale(final_activation)
    final = (final_activation * final_scale * gain_final).astype(jnp.bfloat16)
    logits = jnp.dot(final, head, preferred_element_type=jnp.float32)
    highest = lax.optimization_barrier(jnp.max(logits, axis=1, keepdims=True))
    log_total = highest + jnp.log(lax.optimization_barrier(jnp.sum(jnp.exp(logits - highest), axis=1, keepdims=True)))
    wanted = (targs[:, None] == letters[None, :]).astype(jnp.float32)
    token_loss = log_total[:, 0] - lax.optimization_barrier(jnp.sum(logits * wanted, axis=1))
    probs = jnp.exp(logits - log_total)
    grad_logits = ((probs - wanted) * loss_scale).astype(jnp.bfloat16)
    grad_head = contract_rows(final, grad_logits)
    grad_final = contract_cols(grad_logits, head)
    final_activation_gradient, grad_gain_final = rms_back(final_activation, final_scale, gain_final, grad_final)
    between_blocks_gradient, second_norm_gain_gradient, second_kernel_gradient, second_projection_gradient = residual_block_backward(final_activation_gradient, second_block_residuals, second_norm_gain, second_kernel_weights, second_output_projection, SECOND_DILATION)
    initial_activation_gradient, first_norm_gain_gradient, first_kernel_gradient, first_projection_gradient = residual_block_backward(between_blocks_gradient, first_block_residuals, first_norm_gain, first_kernel_weights, first_output_projection, FIRST_DILATION)
    grad_embed = contract_rows(onehot, initial_activation_gradient.astype(jnp.bfloat16))
    grads = (grad_embed, first_norm_gain_gradient, first_kernel_gradient, first_projection_gradient, second_norm_gain_gradient, second_kernel_gradient, second_projection_gradient, grad_gain_final, grad_head)
    return (token_loss, grads)

def reference(tokens, targets, embed, first_norm_gain, first_kernel_weights, first_output_projection, second_norm_gain, second_kernel_weights, second_output_projection, gain_final, head):
    weights = (embed, first_norm_gain, first_kernel_weights, first_output_projection, second_norm_gain, second_kernel_weights, second_output_projection, gain_final, head)
    loss_scale = float(DOCS * LENGTH) ** (-0.5)

    def step(carry, item):
        losses, grads = one_document(weights, item[0], item[1], loss_scale)
        return (jax.tree.map(lambda total, part: total + part, carry, grads), losses)
    zeros = jax.tree.map(lambda weight: jnp.zeros(weight.shape, jnp.float32), weights)
    totals, losses = lax.scan(step, zeros, (tokens, targets))
    return (losses, totals[0], totals[1], totals[2], totals[3], totals[4], totals[5], totals[6], totals[7], totals[8])
```

```python
import jax
import jax.numpy as jnp
from jax import lax
from jax.sharding import Mesh, PartitionSpec as P

EPS = 1e-05
WIDE = 256
HALF = 2560


def contract_rows(left, right):
    return lax.dot_general(
        left, right, (((0,), (0,)), ((), ())), preferred_element_type=jnp.float32
    )


def contract_cols(left, right):
    return lax.dot_general(
        left, right, (((1,), (1,)), ((), ())), preferred_element_type=jnp.float32
    )


def delay(values, by):
    return jnp.concatenate([jnp.zeros_like(values[:by]), values[:-by]], axis=0)


def advance(values, by):
    return jnp.concatenate([values[by:], jnp.zeros_like(values[:by])], axis=0)


def rms_scale(values):
    return lax.rsqrt(jnp.mean(values * values, axis=-1, keepdims=True) + EPS)


def rms_back(values, scale, gain, grad_out):
    weighted = grad_out * gain
    grad_in = scale * weighted - values * scale**3 * jnp.mean(
        weighted * values, axis=-1, keepdims=True
    )
    grad_gain = jnp.sum(grad_out * values * scale, axis=0)
    return (grad_in, grad_gain)


def residual_block_forward(values, gain, taps, out_w, step):
    scale = rms_scale(values)
    normed = values * scale * gain
    hidden = jnp.maximum(normed, 0.0).astype(jnp.bfloat16)
    stacked = jnp.concatenate([hidden, delay(hidden, step), delay(hidden, 2 * step)], axis=1)
    conv = jnp.dot(stacked, taps.reshape(-1, taps.shape[2]), preferred_element_type=jnp.float32)
    active = jnp.maximum(conv, 0.0).astype(jnp.bfloat16)
    result = values + jnp.dot(active, out_w, preferred_element_type=jnp.float32)
    return (result, (values, scale, normed, stacked, conv, active))


def residual_block_backward(grad_out, saved, gain, taps, out_w, step):
    values, scale, normed, stacked, conv, active = saved
    width = values.shape[1]
    grad_low = grad_out.astype(jnp.bfloat16)
    grad_out_w = contract_rows(active, grad_low)
    grad_active = contract_cols(grad_low, out_w)
    grad_conv = jnp.where(conv > 0, grad_active, 0.0).astype(jnp.bfloat16)
    grad_taps = contract_rows(stacked, grad_conv).reshape(taps.shape)
    returns = contract_cols(grad_conv, taps.reshape(-1, taps.shape[2])).astype(jnp.bfloat16)
    grad_hidden = (
        returns[:, :width].astype(jnp.float32)
        + advance(returns[:, width : 2 * width], step).astype(jnp.float32)
        + advance(returns[:, 2 * width :], 2 * step).astype(jnp.float32)
    )
    grad_normed = jnp.where(normed > 0, grad_hidden, 0.0)
    grad_in, grad_gain = rms_back(values, scale, gain, grad_normed)
    return (grad_out + grad_in, grad_gain, grad_taps, grad_out_w)


def pick(array, index):
    return lax.dynamic_index_in_dim(array, index, 0, keepdims=False)


def swap(array, axis, mask):
    count = lax.axis_size(axis)
    return lax.ppermute(array, axis, [(i, i ^ mask) for i in range(count)])


def scatter_sum(array, axis, dtype):
    count = lax.axis_size(axis)
    mine = lax.axis_index(axis)
    parts = array.reshape(count, -1, WIDE)
    total = pick(parts, mine)
    for k in range(1, count):
        sent = pick(parts, lax.rem(mine + k, count)).astype(dtype)
        got = lax.ppermute(sent, axis, [(i, (i + k) % count) for i in range(count)])
        total = total + got.astype(jnp.float32)
    return total


def gather(array, axis):
    count = lax.axis_size(axis)
    mine = lax.axis_index(axis)
    whole = jnp.zeros((count,) + array.shape, array.dtype)
    whole = lax.dynamic_update_index_in_dim(whole, array, mine, 0)
    for k in range(1, count):
        got = lax.ppermute(array, axis, [(i, (i + k) % count) for i in range(count)])
        whole = lax.dynamic_update_index_in_dim(whole, got, lax.rem(mine + count - k, count), 0)
    return whole.reshape(-1, WIDE)


X = ("x_hi", "x_lo")


def reduce_all(first, second):
    core = lax.axis_index("core")
    keep = jnp.where(core == 0, first, second)
    send = jnp.where(core == 0, second, first)
    total = keep + swap(send, "core", 1)
    total = scatter_sum(total, X, jnp.bfloat16)
    total = scatter_sum(total, "y", jnp.bfloat16)
    bit = lax.rem(lax.axis_index("z"), 2)
    pair = total.reshape(2, -1, WIDE)
    total = pick(pair, bit) + swap(pick(pair, 1 - bit), "z", 1)
    total = total + swap(total, "z", 2)
    total = total + swap(total, "z", 4)
    total = total.astype(jnp.bfloat16)
    other = swap(total, "z", 1)
    total = jnp.where(bit == 0, jnp.concatenate([total, other]), jnp.concatenate([other, total]))
    total = gather(total, "y")
    total = gather(total, X)
    other = swap(total, "core", 1)
    return jnp.where(core == 0, total, other), jnp.where(core == 0, other, total)


def local(
    tokens,
    targets,
    embed,
    first_norm_gain,
    first_kernel_weights,
    first_output_projection,
    second_norm_gain,
    second_kernel_weights,
    second_output_projection,
    gain_final,
    head,
):
    ctx = ("x_lo", "y", "z")
    shards = lax.axis_size(ctx)
    count = tokens.shape[1]
    step = count // shards
    loss_scale = float(count * shards * lax.axis_size(("x_hi", "core"))) ** (-0.5)
    both = jnp.concatenate([tokens.reshape(shards, step), targets.reshape(shards, step)], axis=1)
    both = lax.all_to_all(both, ctx, 0, 0, tiled=True)
    toks = both[:, :step].reshape(-1)
    targs = both[:, step:].reshape(-1)
    letters = jnp.arange(embed.shape[0], dtype=jnp.int32)
    onehot = (toks[:, None] == letters[None, :]).astype(jnp.bfloat16)
    initial = jnp.dot(onehot, embed, preferred_element_type=jnp.float32)
    between, first_saved = residual_block_forward(
        initial, first_norm_gain, first_kernel_weights, first_output_projection, step
    )
    last, second_saved = residual_block_forward(
        between, second_norm_gain, second_kernel_weights, second_output_projection, 2 * step
    )
    final_scale = rms_scale(last)
    final = (last * final_scale * gain_final).astype(jnp.bfloat16)
    logits = jnp.dot(final, head, preferred_element_type=jnp.float32)
    highest = jnp.max(logits, axis=1, keepdims=True)
    log_total = highest + jnp.log(jnp.sum(jnp.exp(logits - highest), axis=1, keepdims=True))
    wanted = (targs[:, None] == letters[None, :]).astype(jnp.float32)
    token_loss = log_total[:, 0] - jnp.sum(logits * wanted, axis=1)
    token_loss = lax.all_to_all(token_loss.reshape(shards, step), ctx, 0, 0, tiled=True)
    probs = jnp.exp(logits - log_total)
    grad_logits = ((probs - wanted) * loss_scale).astype(jnp.bfloat16)
    grad_head = contract_rows(final, grad_logits)
    grad_final = contract_cols(grad_logits, head)
    grad_last, grad_gain_final = rms_back(last, final_scale, gain_final, grad_final)
    grad_between, second_gain_grad, second_taps_grad, second_out_grad = residual_block_backward(
        grad_last,
        second_saved,
        second_norm_gain,
        second_kernel_weights,
        second_output_projection,
        2 * step,
    )
    grad_initial, first_gain_grad, first_taps_grad, first_out_grad = residual_block_backward(
        grad_between,
        first_saved,
        first_norm_gain,
        first_kernel_weights,
        first_output_projection,
        step,
    )
    grad_embed = contract_rows(onehot, grad_initial.astype(jnp.bfloat16))

    def pack(square, taps, out_w, gains):
        rows = jnp.concatenate([square, taps.reshape(-1, WIDE), out_w] + [g[None] for g in gains])
        return jnp.pad(rows, ((0, HALF - rows.shape[0]), (0, 0)))

    first = pack(grad_embed, first_taps_grad, first_out_grad, [first_gain_grad])
    second = pack(grad_head, second_taps_grad, second_out_grad, [second_gain_grad, grad_gain_final])
    first, second = reduce_all(first, second)

    def unpack(rows):
        rows = rows.astype(jnp.float32)
        return rows[:256], rows[256:1792].reshape(3, 256, 512), rows[1792:2304], rows[2304], rows[2305]

    grad_embed, first_taps_grad, first_out_grad, first_gain_grad, _ = unpack(first)
    grad_head, second_taps_grad, second_out_grad, second_gain_grad, grad_gain_final = unpack(second)
    return (
        token_loss.reshape(1, count),
        grad_embed,
        first_gain_grad,
        first_taps_grad,
        first_out_grad,
        second_gain_grad,
        second_taps_grad,
        second_out_grad,
        grad_gain_final,
        grad_head,
    )


def solution(mesh):
    fine = Mesh(mesh.devices.reshape(2, 2, 2, 4, 8), ("x_hi", "core", "x_lo", "y", "z"))
    data = P(("x_hi", "core"), ("x_lo", "y", "z"))
    in_specs = (data, data, P(), P(), P(), P(), P(), P(), P(), P(), P())
    out_specs = (data, P(), P(), P(), P(), P(), P(), P(), P(), P())
    return jax.shard_map(local, mesh=fine, in_specs=in_specs, out_specs=out_specs, check_vma=False)
```

```python
import functools

import jax
import jax.numpy as jnp
from jax import lax
from jax.experimental import pallas as pl
from jax.experimental.pallas import tpu as pltpu
from jax.sharding import Mesh, PartitionSpec as P

EPS = 1e-05
BF = jnp.bfloat16
F32 = jnp.float32
WIDE = 256
HALF = 2560
LEAD = 128
CHUNK = 1024


def rows_dot(left, right):
    return lax.dot_general(left, right, (((0,), (0,)), ((), ())), preferred_element_type=F32)

def cols_dot(left, right):
    return lax.dot_general(left, right, (((1,), (1,)), ((), ())), preferred_element_type=F32)

def dot(left, right):
    return jnp.dot(left, right, preferred_element_type=F32)

def mean(v):
    return jnp.sum(v, axis=-1, keepdims=True) * (1.0 / WIDE)

def kernel(step, chunk, loss_scale, core_ref, toks_ref, targs_ref, embed_ref, gain1_ref, taps1_ref, out1_ref, gain2_ref, taps2_ref,
           out2_ref, gainf_ref, head_ref, loss_ref, keep_ref,
           x0_ref, h1_ref, a1_ref, x1_ref, h2_ref, a2_ref, gx2_ref, gc2_ref, gc1_ref, lossT_ref):
    rows = x0_ref.shape[0]
    n = rows // chunk
    blocks = chunk // 128
    core = core_ref[0]
    one = core
    two = 1 - core
    zeros = jnp.zeros((LEAD, WIDE), BF)
    h1_ref[0:LEAD, :] = zeros
    h2_ref[0:LEAD, :] = zeros
    gc1_ref[rows:rows + LEAD, :] = jnp.zeros((LEAD, 2 * WIDE), BF)
    gc2_ref[rows:rows + LEAD, :] = jnp.zeros((LEAD, 2 * WIDE), BF)
    keep_ref[...] = jnp.zeros_like(keep_ref)
    tokT = toks_ref[...].T
    targT = targs_ref[...].T
    letters = lax.broadcasted_iota(jnp.int32, (128, WIDE), 1)
    column = lax.broadcasted_iota(jnp.int32, tokT.shape, 1)

    def choose(table, i):
        cols = [jnp.sum(jnp.where(column == i * blocks + b, table, 0), axis=1, keepdims=True) for b in range(blocks)]
        return cols

    def forward(i, carry):
        t0 = pl.multiple_of(i * chunk, chunk)
        here = pl.ds(t0, chunk)
        onehot = jnp.concatenate([(c == letters).astype(F32).astype(BF) for c in choose(tokT, i)], axis=0)
        x0 = dot(onehot, embed_ref[...])
        x0_ref[here, :] = x0.astype(BF)
        s = lax.rsqrt(mean(x0 * x0) + EPS)
        h = jnp.maximum(x0 * s * gain1_ref[...], 0.0).astype(BF)
        h1_ref[pl.ds(t0 + LEAD, chunk), :] = h
        hs = jnp.concatenate([h, h1_ref[pl.ds(t0 + LEAD - step, chunk), :], h1_ref[pl.ds(t0 + LEAD - 2 * step, chunk), :]], axis=1)
        a = jnp.maximum(dot(hs, taps1_ref[...]), 0.0).astype(BF)
        a1_ref[here, :] = a
        x1 = x0 + dot(a, out1_ref[...])
        x1_ref[here, :] = x1
        s = lax.rsqrt(mean(x1 * x1) + EPS)
        h = jnp.maximum(x1 * s * gain2_ref[...], 0.0).astype(BF)
        h2_ref[pl.ds(t0 + LEAD, chunk), :] = h
        hs = jnp.concatenate([h, h2_ref[pl.ds(t0 + LEAD - 2 * step, chunk), :], h2_ref[pl.ds(t0 + LEAD - 4 * step, chunk), :]], axis=1)
        a = jnp.maximum(dot(hs, taps2_ref[...]), 0.0).astype(BF)
        a2_ref[here, :] = a
        x2 = x1 + dot(a, out2_ref[...])
        s = lax.rsqrt(mean(x2 * x2) + EPS)
        normed = x2 * s
        final = (normed * gainf_ref[...]).astype(BF)
        logits = dot(final, head_ref[...])
        highest = jnp.max(logits, axis=1, keepdims=True)
        e = jnp.exp(logits - highest)
        total = jnp.sum(e, axis=1, keepdims=True)
        wanted = jnp.concatenate([(c == letters).astype(F32) for c in choose(targT, i)], axis=0)
        loss = highest + jnp.log(total) - jnp.sum(logits * wanted, axis=1, keepdims=True)
        place = lax.broadcasted_iota(jnp.int32, lossT_ref.shape, 1)
        for b in range(blocks):
            lossT_ref[...] = jnp.where(place == i * blocks + b, loss[b * 128:(b + 1) * 128], lossT_ref[...])
        gl = ((e * (1.0 / total) - wanted) * loss_scale).astype(BF)
        keep_ref[two, 0:256, :] += rows_dot(final, gl)
        gfin = cols_dot(gl, head_ref[...])
        keep_ref[two, 2305:2306, :] += jnp.sum(gfin * normed, axis=0, keepdims=True)
        w = gfin * gainf_ref[...]
        gx2 = s * (w - normed * mean(w * normed))
        gx2_ref[here, :] = gx2
        low = gx2.astype(BF)
        keep_ref[two, 1792:2304, :] += rows_dot(a, low)
        gact = cols_dot(low, out2_ref[...])
        gc2_ref[here, :] = jnp.where(a > 0, gact, 0.0).astype(BF)
        return carry

    lax.fori_loop(0, n, forward, 0)
    loss_ref[...] = lossT_ref[...].T

    def back(i, carry):
        j = n - 1 - i
        t0 = pl.multiple_of(j * chunk, chunk)
        here = pl.ds(t0, chunk)

        def block(g, x, h, gc_ref, slot, taps_ref, gain, dist):
            gcs = [gc_ref[pl.ds(t0 + k * dist, chunk), :] for k in range(3)]
            gh = sum(cols_dot(gcs[k], taps_ref[k * WIDE:(k + 1) * WIDE, :]) for k in range(3))
            for k in range(3):
                part = rows_dot(h, gcs[k])
                keep_ref[slot, 256 + 512 * k:512 + 512 * k, :] += part[:, :WIDE]
                keep_ref[slot, 512 + 512 * k:768 + 512 * k, :] += part[:, WIDE:]
            gn = jnp.where(h > 0, gh, 0.0)
            s = lax.rsqrt(mean(x * x) + EPS)
            normed = x * s
            keep_ref[slot, 2304:2305, :] += jnp.sum(gn * normed, axis=0, keepdims=True)
            w = gn * gain
            return g + s * (w - normed * mean(w * normed))

        gx1 = block(gx2_ref[here, :], x1_ref[here, :], h2_ref[pl.ds(t0 + LEAD, chunk), :], gc2_ref, two, taps2_ref, gain2_ref[...], 2 * step)
        low = gx1.astype(BF)
        a = a1_ref[here, :]
        keep_ref[one, 1792:2304, :] += rows_dot(a, low)
        gact = cols_dot(low, out1_ref[...])
        gc1_ref[here, :] = jnp.where(a > 0, gact, 0.0).astype(BF)
        gx0 = block(gx1, x0_ref[here, :].astype(F32), h1_ref[pl.ds(t0 + LEAD, chunk), :], gc1_ref, one, taps1_ref, gain1_ref[...], step)
        up = lax.broadcasted_iota(jnp.int32, (WIDE, 128), 0)
        toks_here = toks_ref[pl.ds(j * blocks, blocks), :]
        onehotT = jnp.concatenate([(up == toks_here[b:b + 1, :]).astype(F32).astype(BF) for b in range(blocks)], axis=1)
        keep_ref[one, 0:256, :] += dot(onehotT, gx0.astype(BF))
        return carry

    lax.fori_loop(0, n, back, 0)


def compute(core, toks, targs, embed, g1, taps1, out1, g2, taps2, out2, gf, head, loss_scale, step, chunk=CHUNK):
    rows = toks.size
    vm = lambda *s: pltpu.VMEM(s[:-1], s[-1])
    return pl.pallas_call(
        functools.partial(kernel, step, chunk, loss_scale),
        out_shape=(jax.ShapeDtypeStruct((rows // 128, 128), F32), jax.ShapeDtypeStruct((2, HALF, WIDE), F32)),
        in_specs=[pl.BlockSpec(memory_space=pltpu.SMEM)] + [pl.BlockSpec(memory_space=pltpu.VMEM)] * 11,
        out_specs=(pl.BlockSpec(memory_space=pltpu.VMEM), pl.BlockSpec(memory_space=pltpu.VMEM)),
        scratch_shapes=[
            vm(rows, WIDE, BF), vm(rows + LEAD, WIDE, BF), vm(rows, 2 * WIDE, BF), vm(rows, WIDE, F32),
            vm(rows + LEAD, WIDE, BF), vm(rows, 2 * WIDE, BF), vm(rows, WIDE, F32), vm(rows + LEAD, 2 * WIDE, BF),
            vm(rows + LEAD, 2 * WIDE, BF), vm(128, rows // 128, F32),
        ],
        compiler_params=pltpu.CompilerParams(vmem_limit_bytes=50 * 2**20),
    )(core, toks.reshape(-1, 128), targs.reshape(-1, 128), embed, g1[None], taps1.reshape(-1, 512), out1, g2[None], taps2.reshape(-1, 512), out2, gf[None], head)


def pick(array, index):
    return lax.dynamic_index_in_dim(array, index, 0, keepdims=False)


def swap(array, axis, mask):
    count = lax.axis_size(axis)
    return lax.ppermute(array, axis, [(i, i ^ mask) for i in range(count)])


def scatter_sum(array, axis, dtype):
    count = lax.axis_size(axis)
    mine = lax.axis_index(axis)
    parts = array.reshape(count, -1, WIDE)
    total = pick(parts, mine)
    for k in range(1, count):
        sent = pick(parts, lax.rem(mine + k, count)).astype(dtype)
        got = lax.ppermute(sent, axis, [(i, (i + k) % count) for i in range(count)])
        total = total + got.astype(jnp.float32)
    return total


def gather(array, axis):
    count = lax.axis_size(axis)
    mine = lax.axis_index(axis)
    whole = jnp.zeros((count,) + array.shape, array.dtype)
    whole = lax.dynamic_update_index_in_dim(whole, array, mine, 0)
    for k in range(1, count):
        got = lax.ppermute(array, axis, [(i, (i + k) % count) for i in range(count)])
        whole = lax.dynamic_update_index_in_dim(whole, got, lax.rem(mine + count - k, count), 0)
    return whole.reshape(-1, WIDE)


X = ("x_hi", "x_lo")


def reduce_all(keep, send):
    total = keep + swap(send, "core", 1)
    total = scatter_sum(total, X, BF)
    total = scatter_sum(total, "y", BF)
    bit = lax.rem(lax.axis_index("z"), 2)
    pair = total.reshape(2, -1, WIDE)
    total = pick(pair, bit) + swap(pick(pair, 1 - bit), "z", 1)
    total = total + swap(total, "z", 2)
    total = total + swap(total, "z", 4)
    total = total.astype(BF)
    other = swap(total, "z", 1)
    total = jnp.where(bit == 0, jnp.concatenate([total, other]), jnp.concatenate([other, total]))
    total = gather(total, "y")
    total = gather(total, X)
    return total, swap(total, "core", 1)


def spread_kernel(core_ref, mine_ref, other_ref, *outs):
    even = core_ref[0] == 0

    def write(first, square, taps, out_w, gains):
        def rows(start, count):
            left, right = mine_ref[pl.ds(start, count), :], other_ref[pl.ds(start, count), :]
            return (jnp.where(even, left, right) if first else jnp.where(even, right, left)).astype(F32)

        square[...] = rows(0, 256)
        for k in range(3):
            taps[k, :, :WIDE] = rows(256 + 512 * k, 256)
            taps[k, :, WIDE:] = rows(512 + 512 * k, 256)
        out_w[...] = rows(1792, 512)
        tail = rows(2304, 16)
        for i, gain in enumerate(gains):
            gain[...] = tail[i : i + 1]

    embed, gain1, taps1, out1, gain2, taps2, out2, gainf, head = outs
    write(True, embed, taps1, out1, [gain1])
    write(False, head, taps2, out2, [gain2, gainf])


def spread(core, mine, other):
    vmem = pl.BlockSpec(memory_space=pltpu.VMEM)
    shapes = [(256, 256), (1, 256), (3, 256, 512), (512, 256), (1, 256), (3, 256, 512), (512, 256), (1, 256), (256, 256)]
    return pl.pallas_call(
        spread_kernel,
        out_shape=tuple(jax.ShapeDtypeStruct(s, F32) for s in shapes),
        in_specs=[pl.BlockSpec(memory_space=pltpu.SMEM), vmem, vmem],
        out_specs=(vmem,) * len(shapes),
        compiler_params=pltpu.CompilerParams(vmem_limit_bytes=32 * 2**20),
    )(core, mine, other)


def local(
    tokens,
    targets,
    embed,
    first_norm_gain,
    first_kernel_weights,
    first_output_projection,
    second_norm_gain,
    second_kernel_weights,
    second_output_projection,
    gain_final,
    head,
):
    ctx = ("x_lo", "y", "z")
    shards = lax.axis_size(ctx)
    count = tokens.shape[1]
    step = count // shards
    loss_scale = float(count * shards * lax.axis_size(("x_hi", "core"))) ** (-0.5)
    both = jnp.concatenate([tokens.reshape(shards, step), targets.reshape(shards, step)], axis=1)
    both = lax.all_to_all(both, ctx, 0, 0, tiled=True)
    core = lax.axis_index("core").reshape(1)
    loss, packed = compute(
        core,
        both[:, :step],
        both[:, step:],
        embed,
        first_norm_gain,
        first_kernel_weights,
        first_output_projection,
        second_norm_gain,
        second_kernel_weights,
        second_output_projection,
        gain_final,
        head,
        loss_scale,
        step,
    )
    loss = lax.all_to_all(loss.reshape(shards, step), ctx, 0, 0, tiled=True)
    mine, other = reduce_all(packed[0], packed[1])
    grad_embed, gain1, taps1, out1, gain2, taps2, out2, gainf, grad_head = spread(core, mine, other)
    return (
        loss.reshape(1, count),
        grad_embed,
        gain1[0],
        taps1,
        out1,
        gain2[0],
        taps2,
        out2,
        gainf[0],
        grad_head,
    )


def solution(mesh):
    fine = Mesh(mesh.devices.reshape(2, 2, 2, 4, 8), ("x_hi", "core", "x_lo", "y", "z"))
    data = P(("x_hi", "core"), ("x_lo", "y", "z"))
    in_specs = (data, data, P(), P(), P(), P(), P(), P(), P(), P(), P())
    out_specs = (data, P(), P(), P(), P(), P(), P(), P(), P(), P())
    return jax.shard_map(local, mesh=fine, in_specs=in_specs, out_specs=out_specs, check_vma=False)
```

```python
import functools

import jax
import jax.numpy as jnp
from jax import lax
from jax.experimental import pallas as pl
from jax.experimental.pallas import tpu as pltpu
from jax.sharding import Mesh, PartitionSpec as P

EPS = 1e-05
BF = jnp.bfloat16
F32 = jnp.float32
WIDE = 256
LANES = 128
LEAD = 128
CHUNK = 1024
STEP = 32
PART = 40
TAPS_AT, OUT_AT, GAINS_AT = 512, 3584, 4608
X = ("x_hi", "x_lo")


def rows_dot(left, right):
    return lax.dot_general(left, right, (((0,), (0,)), ((), ())), preferred_element_type=F32)


def cols_dot(left, right):
    return lax.dot_general(left, right, (((1,), (1,)), ((), ())), preferred_element_type=F32)


def dot(left, right):
    return jnp.dot(left, right, preferred_element_type=F32)


def mean(values):
    return jnp.sum(values, axis=-1, keepdims=True) * (1.0 / WIDE)


def kernel(
    peers,
    loss_scale,
    both_ref,
    embed_hbm,
    gain1_hbm,
    taps1_hbm,
    out1_hbm,
    gain2_hbm,
    taps2_hbm,
    out2_hbm,
    gainf_hbm,
    head_hbm,
    loss_ref,
    *rest,
):
    part = peers * PART
    keep_refs, send_refs = rest[:4], rest[4:8]
    (embed_ref, gain1_ref, taps1_ref, out1_ref, gain2_ref, taps2_ref, out2_ref, gainf_ref, head_ref) = rest[8:17]
    (sems, tok_ref, targ_ref, hot_ref, x0_ref, h1_ref, a1_ref, x1_ref, h2_ref, a2_ref, gx2_ref, gc2_ref, gc1_ref) = rest[17:30]
    losses_ref, acc_ref = rest[30:]
    sources = (embed_hbm, gain1_hbm, taps1_hbm, out1_hbm, gain2_hbm, taps2_hbm, out2_hbm, gainf_hbm, head_hbm)
    copies = [pltpu.make_async_copy(src, dst, sems.at[i]) for i, (src, dst) in enumerate(zip(sources, rest[8:17]))]
    for copy in copies:
        copy.start()
    rows = x0_ref.shape[0]
    n = rows // CHUNK
    shards = CHUNK // STEP
    zeros = jnp.zeros((LEAD, WIDE), BF)
    h1_ref[0:LEAD, :] = zeros
    h2_ref[0:LEAD, :] = zeros
    gc1_ref[rows : rows + LEAD, :] = jnp.zeros((LEAD, 2 * WIDE), BF)
    gc2_ref[rows : rows + LEAD, :] = jnp.zeros((LEAD, 2 * WIDE), BF)
    acc_ref[...] = jnp.zeros_like(acc_ref)
    quarter = lax.rem(lax.axis_index("z"), 4)

    def mine(block):
        pieces = [block[:, STEP * p : STEP * (p + 1)] for p in range(4)]
        low = jnp.where(quarter == 0, pieces[0], pieces[1])
        high = jnp.where(quarter == 2, pieces[2], pieces[3])
        return jnp.where(quarter < 2, low, high)

    tok_ref[...] = mine(both_ref[:, 0, :])
    targ_ref[...] = mine(both_ref[:, 1, :])
    letters = lax.broadcasted_iota(jnp.int32, (CHUNK, WIDE), 1)
    diagonal = lax.rem(lax.broadcasted_iota(jnp.int32, (CHUNK, STEP), 0), STEP) == lax.broadcasted_iota(
        jnp.int32, (CHUNK, STEP), 1
    )

    def column(ref, i):
        block = ref[pl.ds(pl.multiple_of(i * shards, shards), shards), :]
        tall = jnp.broadcast_to(block[:, None, :], (shards, STEP, STEP)).reshape(CHUNK, STEP)
        return jnp.sum(jnp.where(diagonal, tall, 0), axis=1, keepdims=True)

    def add(half, at, value):
        height = value.shape[0]
        for b in range(value.shape[1] // LANES):
            start = at + b * height
            acc_ref[half, start : start + height, :] += value[:, b * LANES : (b + 1) * LANES]

    for copy in copies:
        copy.wait()

    def forward(i, carry):
        t0 = pl.multiple_of(i * CHUNK, CHUNK)
        here = pl.ds(t0, CHUNK)
        onehot = (column(tok_ref, i) == letters).astype(F32).astype(BF)
        hot_ref[here, :] = onehot
        x0 = dot(onehot, embed_ref[...])
        x0_ref[here, :] = x0.astype(BF)

        def layer(x, gain_ref, taps_ref, out_ref, h_ref, a_ref, dist):
            s = lax.rsqrt(mean(x * x) + EPS)
            h = jnp.maximum(x * s * gain_ref[...], 0.0).astype(BF)
            h_ref[pl.ds(t0 + LEAD, CHUNK), :] = h
            near = h_ref[pl.ds(t0 + LEAD - dist, CHUNK), :]
            far = h_ref[pl.ds(t0 + LEAD - 2 * dist, CHUNK), :]
            a = jnp.maximum(dot(jnp.concatenate([h, near, far], axis=1), taps_ref[...]), 0.0).astype(BF)
            a_ref[here, :] = a
            return x + dot(a, out_ref[...]), a

        x1, _ = layer(x0, gain1_ref, taps1_ref, out1_ref, h1_ref, a1_ref, STEP)
        x1_ref[here, :] = x1
        x2, a = layer(x1, gain2_ref, taps2_ref, out2_ref, h2_ref, a2_ref, 2 * STEP)
        s = lax.rsqrt(mean(x2 * x2) + EPS)
        normed = x2 * s
        final = (normed * gainf_ref[...]).astype(BF)
        logits = dot(final, head_ref[...])
        highest = jnp.max(logits, axis=1, keepdims=True)
        e = jnp.exp(logits - highest)
        total = jnp.sum(e, axis=1, keepdims=True)
        wanted = (column(targ_ref, i) == letters).astype(F32)
        loss = highest + jnp.log(total) - jnp.sum(logits * wanted, axis=1, keepdims=True)
        spread = jnp.where(diagonal, loss, 0.0).reshape(shards, STEP, STEP)
        losses_ref[pl.ds(pl.multiple_of(i * shards, shards), shards), :] = jnp.sum(spread, axis=1)
        gl = ((e * (1.0 / total) - wanted) * loss_scale).astype(BF)
        add(1, 0, rows_dot(final, gl))
        gfin = cols_dot(gl, head_ref[...])
        add(1, GAINS_AT + 2, jnp.sum(gfin * normed, axis=0, keepdims=True))
        w = gfin * gainf_ref[...]
        gx2 = s * (w - normed * mean(w * normed))
        gx2_ref[here, :] = gx2
        low = gx2.astype(BF)
        add(1, OUT_AT, rows_dot(a, low))
        gact = cols_dot(low, out2_ref[...])
        gc2_ref[here, :] = jnp.where(a > 0, gact, 0.0).astype(BF)
        return carry

    lax.fori_loop(0, n, forward, 0)

    losses = losses_ref[...]
    high = losses.astype(BF).astype(F32)
    low = losses - high
    half = peers
    loss_ref[...] = jnp.concatenate([high[:half], low[:half], high[half:], low[half:]], axis=1).astype(BF)

    def back(i, carry):
        j = n - 1 - i
        t0 = pl.multiple_of(j * CHUNK, CHUNK)
        here = pl.ds(t0, CHUNK)

        def block(g, x, h, gc_ref, half, taps_ref, gain, dist):
            gcs = [gc_ref[pl.ds(t0 + k * dist, CHUNK), :] for k in range(3)]
            gh = sum(cols_dot(gcs[k], taps_ref[k * WIDE : (k + 1) * WIDE, :]) for k in range(3))
            for k in range(3):
                add(half, TAPS_AT + 1024 * k, rows_dot(h, gcs[k]))
            gn = jnp.where(h > 0, gh, 0.0)
            s = lax.rsqrt(mean(x * x) + EPS)
            normed = x * s
            add(half, GAINS_AT, jnp.sum(gn * normed, axis=0, keepdims=True))
            w = gn * gain
            return g + s * (w - normed * mean(w * normed))

        h2 = h2_ref[pl.ds(t0 + LEAD, CHUNK), :]
        gx1 = block(gx2_ref[here, :], x1_ref[here, :], h2, gc2_ref, 1, taps2_ref, gain2_ref[...], 2 * STEP)
        low = gx1.astype(BF)
        a = a1_ref[here, :]
        add(0, OUT_AT, rows_dot(a, low))
        gact = cols_dot(low, out1_ref[...])
        gc1_ref[here, :] = jnp.where(a > 0, gact, 0.0).astype(BF)
        h1 = h1_ref[pl.ds(t0 + LEAD, CHUNK), :]
        gx0 = block(gx1, x0_ref[here, :].astype(F32), h1, gc1_ref, 0, taps1_ref, gain1_ref[...], STEP)
        add(0, 0, rows_dot(hot_ref[here, :], gx0.astype(BF)))
        return carry

    lax.fori_loop(0, n, back, 0)

    core, x = lax.axis_index("core"), lax.axis_index(X)
    for k in range(4):
        at = pl.ds(pl.multiple_of(lax.rem(x + k, 4) * part, part), part)
        keep_refs[k][...] = acc_ref[core, at, :]
        send_refs[k][...] = acc_ref[1 - core, at, :]


def compute(both, weights, loss_scale, peers):
    rows = both.shape[0] * STEP
    part = peers * PART
    vmem, hbm = pl.BlockSpec(memory_space=pltpu.VMEM), pl.BlockSpec(memory_space=pltpu.HBM)
    shapes = [(WIDE, BF), (2 * WIDE, BF), (WIDE, F32)]
    tall = lambda wide, dtype, extra=0: pltpu.VMEM((rows + extra, wide), dtype)
    return pl.pallas_call(
        functools.partial(kernel, peers, loss_scale),
        out_shape=[jax.ShapeDtypeStruct((peers, LANES), BF)] + [jax.ShapeDtypeStruct((part, LANES), F32)] * 8,
        in_specs=[vmem] + [hbm] * len(weights),
        out_specs=[vmem] * 9,
        scratch_shapes=[pltpu.VMEM(w.shape, w.dtype) for w in weights]
        + [
            pltpu.SemaphoreType.DMA((len(weights),)),
            pltpu.VMEM((rows // STEP, STEP), jnp.int32),
            pltpu.VMEM((rows // STEP, STEP), jnp.int32),
            tall(WIDE, BF),
            tall(WIDE, BF),
            tall(WIDE, BF, LEAD),
            tall(2 * WIDE, BF),
            tall(WIDE, F32),
            tall(WIDE, BF, LEAD),
            tall(2 * WIDE, BF),
            tall(WIDE, F32),
            tall(2 * WIDE, BF, LEAD),
            tall(2 * WIDE, BF, LEAD),
            pltpu.VMEM((rows // STEP, STEP), F32),
            pltpu.VMEM((2, 4 * part, LANES), F32),
        ],
        compiler_params=pltpu.CompilerParams(vmem_limit_bytes=57 * 2**20),
    )(both, *weights)


def swap(array, axis, mask):
    count = lax.axis_size(axis)
    return lax.ppermute(array, axis, [(i, i ^ mask) for i in range(count)])


def shift(array, axis, by):
    count = lax.axis_size(axis)
    return lax.ppermute(array, axis, [(i, (i + by) % count) for i in range(count)])


def reduce_all(keep, send, loss):
    parts = [mine + swap(other, "core", 1) for mine, other in zip(keep, send)]
    total = parts[0]
    for k in range(1, 4):
        total = total + shift(parts[k].astype(BF), X, k).astype(F32)
    rest = ("y", "z")
    peers = lax.axis_size(rest)
    message = total.astype(BF).reshape(peers, PART, LANES)
    message = jnp.concatenate([message, jnp.broadcast_to(loss[:, None], (peers, 8, LANES))], axis=1)
    got = lax.all_to_all(message, rest, 0, 0, tiled=True)
    loss = got[:, PART]
    summed = jnp.sum(got[:, :PART].astype(F32), axis=0).astype(BF)
    whole = jnp.broadcast_to(summed[None], (peers, PART, LANES))
    whole = lax.all_to_all(whole, rest, 0, 0, tiled=True).reshape(-1, LANES)
    mine = [whole] + [shift(whole, X, k) for k in range(1, 4)]
    return mine, [swap(piece, "core", 1) for piece in mine], loss, swap(loss, "x_lo", 1)


def spread_kernel(*refs):
    mine, others = refs[:4], refs[4:8]
    loss_mine, loss_other = refs[8:10]
    loss_ref, embed, gain1, taps1, out1, gain2, taps2, out2, gainf, head = refs[10:20]
    big, lines = refs[20:]
    core, x, x_lo = lax.axis_index("core"), lax.axis_index(X), lax.axis_index("x_lo")
    part = mine[0].shape[0]
    for k in range(4):
        at = pl.ds(pl.multiple_of(lax.rem(x + 4 - k, 4) * part, part), part)
        big[core, at, :] = mine[k][...]
        big[1 - core, at, :] = others[k][...]

    def write(half, square, taps, out_w, gains):
        def put(target, at, height, count):
            for b in range(count):
                start = at + b * height
                target[:, b * LANES : (b + 1) * LANES] = big[half, start : start + height, :].astype(F32)

        put(square, 0, 256, 2)
        for k in range(3):
            put(taps.at[k], TAPS_AT + 1024 * k, 256, 4)
        put(out_w, OUT_AT, 512, 2)
        tail = big[half, GAINS_AT : GAINS_AT + 16, :].astype(F32)
        for i, gain in enumerate(gains):
            gain[:, :LANES] = tail[2 * i : 2 * i + 1]
            gain[:, LANES:] = tail[2 * i + 1 : 2 * i + 2]

    write(0, embed, taps1, out1, [gain1])
    write(1, head, taps2, out2, [gain2, gainf])

    def joined(ref):
        block = ref[...].astype(F32)
        first = block[:, :STEP] + block[:, STEP : 2 * STEP]
        second = block[:, 2 * STEP : 3 * STEP] + block[:, 3 * STEP :]
        return jnp.where(x_lo == 0, first, second)

    here, there = joined(loss_mine), joined(loss_other)
    half = here.shape[0]
    lines[:half, :] = jnp.where(x_lo == 0, here, there)
    lines[half:, :] = jnp.where(x_lo == 0, there, here)
    for b in range(4):
        loss_ref[:, b * STEP : (b + 1) * STEP] = lines[pl.ds(b, half // 2, stride=4), :]


def spread(mine, others, loss_mine, loss_other):
    vmem = pl.BlockSpec(memory_space=pltpu.VMEM)
    part = mine[0].shape[0]
    peers = loss_mine.shape[0]
    square, taps, out_w, gain = (256, 256), (3, 256, 512), (512, 256), (1, 256)
    shapes = [(peers // 2, LANES), square, gain, taps, out_w, gain, taps, out_w, gain, square]
    return pl.pallas_call(
        spread_kernel,
        out_shape=[jax.ShapeDtypeStruct(s, F32) for s in shapes],
        in_specs=[vmem] * 10,
        out_specs=[vmem] * len(shapes),
        scratch_shapes=[pltpu.VMEM((2, 4 * part, LANES), BF), pltpu.VMEM((2 * peers, STEP), F32)],
        compiler_params=pltpu.CompilerParams(vmem_limit_bytes=32 * 2**20),
    )(*mine, *others, loss_mine, loss_other)


def local(tokens, targets, embed, gain1, taps1, out1, gain2, taps2, out2, gainf, head):
    ctx = ("x_lo", "y", "z")
    count = tokens.shape[1]
    shards = lax.axis_size(ctx)
    loss_scale = float(count * shards * lax.axis_size(("x_hi", "core"))) ** (-0.5)
    lines = jnp.stack([tokens.reshape(-1, LANES), targets.reshape(-1, LANES)], axis=1)
    both = jnp.broadcast_to(lines[:, None], (lines.shape[0], 4, 2, LANES)).reshape(shards, 2, LANES)
    both = lax.all_to_all(both, ctx, 0, 0, tiled=True)
    weights = (
        embed,
        gain1[None],
        taps1.reshape(-1, 512),
        out1,
        gain2[None],
        taps2.reshape(-1, 512),
        out2,
        gainf[None],
        head,
    )
    outs = compute(both, weights, loss_scale, shards // 2)
    mine, others, loss_mine, loss_other = reduce_all(outs[1:5], outs[5:9], outs[0])
    loss, *grads = spread(mine, others, loss_mine, loss_other)
    for i in (1, 4, 7):
        grads[i] = grads[i][0]
    return (loss.reshape(1, count), *grads)


def solution(mesh):
    fine = Mesh(mesh.devices.reshape(2, 2, 2, 4, 8), ("x_hi", "core", "x_lo", "y", "z"))
    data = P(("x_hi", "core"), ("x_lo", "y", "z"))
    in_specs = (data, data, P(), P(), P(), P(), P(), P(), P(), P(), P())
    out_specs = (data, P(), P(), P(), P(), P(), P(), P(), P(), P())
    return jax.shard_map(local, mesh=fine, in_specs=in_specs, out_specs=out_specs, check_vma=False)
```

```python
import functools

import jax
import jax.numpy as jnp
from jax import lax
from jax.experimental import pallas as pl
from jax.experimental.pallas import tpu as pltpu
from jax.sharding import Mesh, PartitionSpec as P

EPS = 1e-05
BF = jnp.bfloat16
F32 = jnp.float32
WIDE = 256
LANES = 128
LEAD = 128
CHUNK = 1024
STEP = 32
PART = 40
TAPS_AT, OUT_AT, GAINS_AT = 512, 3584, 4608
X = ("x_hi", "x_lo")


def rows_dot(left, right):
    return lax.dot_general(left, right, (((0,), (0,)), ((), ())), preferred_element_type=F32)


def cols_dot(left, right):
    return lax.dot_general(left, right, (((1,), (1,)), ((), ())), preferred_element_type=F32)


def dot(left, right):
    return jnp.dot(left, right, preferred_element_type=F32)


def mean(values):
    return jnp.sum(values, axis=-1, keepdims=True) * (1.0 / WIDE)


def kernel(
    peers,
    loss_scale,
    both_ref,
    embed_hbm,
    gain1_hbm,
    taps1_hbm,
    out1_hbm,
    gain2_hbm,
    taps2_hbm,
    out2_hbm,
    gainf_hbm,
    head_hbm,
    loss_ref,
    *rest,
):
    part = peers * PART
    keep_refs, send_refs = rest[:4], rest[4:8]
    (embed_ref, gain1_ref, taps1_ref, out1_ref, gain2_ref, taps2_ref, out2_ref, gainf_ref, head_ref) = rest[8:17]
    (sems, tok_ref, targ_ref, hot_ref, x0_ref, h1_ref, a1_ref, x1_ref, h2_ref, a2_ref, gx2_ref, gc2_ref, gc1_ref) = rest[17:30]
    losses_ref, acc_ref = rest[30:]
    sources = (embed_hbm, gain1_hbm, taps1_hbm, out1_hbm, gain2_hbm, taps2_hbm, out2_hbm, gainf_hbm, head_hbm)
    copies = [pltpu.make_async_copy(src, dst, sems.at[i]) for i, (src, dst) in enumerate(zip(sources, rest[8:17]))]
    for copy in copies:
        copy.start()
    rows = x0_ref.shape[0]
    n = rows // CHUNK
    shards = CHUNK // STEP
    zeros = jnp.zeros((LEAD, WIDE), BF)
    h1_ref[0:LEAD, :] = zeros
    h2_ref[0:LEAD, :] = zeros
    gc1_ref[rows : rows + LEAD, :] = jnp.zeros((LEAD, 2 * WIDE), BF)
    gc2_ref[rows : rows + LEAD, :] = jnp.zeros((LEAD, 2 * WIDE), BF)
    acc_ref[...] = jnp.zeros_like(acc_ref)
    quarter = lax.rem(lax.axis_index("z"), 4)

    def mine(block):
        pieces = [block[:, STEP * p : STEP * (p + 1)] for p in range(4)]
        low = jnp.where(quarter == 0, pieces[0], pieces[1])
        high = jnp.where(quarter == 2, pieces[2], pieces[3])
        return jnp.where(quarter < 2, low, high)

    tok_ref[...] = mine(both_ref[:, 0, :])
    targ_ref[...] = mine(both_ref[:, 1, :])
    letters = lax.broadcasted_iota(jnp.int32, (CHUNK, WIDE), 1)
    diagonal = lax.rem(lax.broadcasted_iota(jnp.int32, (CHUNK, STEP), 0), STEP) == lax.broadcasted_iota(
        jnp.int32, (CHUNK, STEP), 1
    )

    def column(ref, i):
        block = ref[pl.ds(pl.multiple_of(i * shards, shards), shards), :]
        tall = jnp.broadcast_to(block[:, None, :], (shards, STEP, STEP)).reshape(CHUNK, STEP)
        return jnp.sum(jnp.where(diagonal, tall, 0), axis=1, keepdims=True)

    def add(half, at, value):
        height = value.shape[0]
        for b in range(value.shape[1] // LANES):
            start = at + b * height
            acc_ref[half, start : start + height, :] += value[:, b * LANES : (b + 1) * LANES]

    for copy in copies:
        copy.wait()

    def forward(i, carry):
        t0 = pl.multiple_of(i * CHUNK, CHUNK)
        here = pl.ds(t0, CHUNK)
        onehot = (column(tok_ref, i) == letters).astype(F32).astype(BF)
        hot_ref[here, :] = onehot
        x0 = dot(onehot, embed_ref[...])
        x0_ref[here, :] = x0.astype(BF)

        def layer(x, gain_ref, taps_ref, out_ref, h_ref, a_ref, dist):
            s = lax.rsqrt(mean(x * x) + EPS)
            h = jnp.maximum(x * s * gain_ref[...], 0.0).astype(BF)
            h_ref[pl.ds(t0 + LEAD, CHUNK), :] = h
            near = h_ref[pl.ds(t0 + LEAD - dist, CHUNK), :]
            far = h_ref[pl.ds(t0 + LEAD - 2 * dist, CHUNK), :]
            a = jnp.maximum(dot(jnp.concatenate([h, near, far], axis=1), taps_ref[...]), 0.0).astype(BF)
            a_ref[here, :] = a
            return x + dot(a, out_ref[...]), a

        x1, _ = layer(x0, gain1_ref, taps1_ref, out1_ref, h1_ref, a1_ref, STEP)
        x1_ref[here, :] = x1
        x2, a = layer(x1, gain2_ref, taps2_ref, out2_ref, h2_ref, a2_ref, 2 * STEP)
        s = lax.rsqrt(mean(x2 * x2) + EPS)
        normed = x2 * s
        final = (normed * gainf_ref[...]).astype(BF)
        logits = dot(final, head_ref[...])
        highest = jnp.max(logits, axis=1, keepdims=True)
        e = jnp.exp(logits - highest)
        total = jnp.sum(e, axis=1, keepdims=True)
        wanted = (column(targ_ref, i) == letters).astype(F32)
        loss = highest + jnp.log(total) - jnp.sum(logits * wanted, axis=1, keepdims=True)
        spread = jnp.where(diagonal, loss, 0.0).reshape(shards, STEP, STEP)
        losses_ref[pl.ds(pl.multiple_of(i * shards, shards), shards), :] = jnp.sum(spread, axis=1)
        gl = ((e * (1.0 / total) - wanted) * loss_scale).astype(BF)
        add(1, 0, rows_dot(final, gl))
        gfin = cols_dot(gl, head_ref[...])
        add(1, GAINS_AT + 2, jnp.sum(gfin * normed, axis=0, keepdims=True))
        w = gfin * gainf_ref[...]
        gx2 = s * (w - normed * mean(w * normed))
        gx2_ref[here, :] = gx2
        low = gx2.astype(BF)
        add(1, OUT_AT, rows_dot(a, low))
        gact = cols_dot(low, out2_ref[...])
        gc2_ref[here, :] = jnp.where(a > 0, gact, 0.0).astype(BF)
        return carry

    lax.fori_loop(0, n, forward, 0)

    losses = losses_ref[...]
    high = losses.astype(BF).astype(F32)
    low = losses - high
    half = peers
    loss_ref[...] = jnp.concatenate([high[:half], low[:half], high[half:], low[half:]], axis=1).astype(BF)

    def back(i, carry):
        j = n - 1 - i
        t0 = pl.multiple_of(j * CHUNK, CHUNK)
        here = pl.ds(t0, CHUNK)

        def block(g, x, h, gc_ref, half, taps_ref, gain, dist):
            gcs = [gc_ref[pl.ds(t0 + k * dist, CHUNK), :] for k in range(3)]
            side = jnp.concatenate(gcs, axis=1)
            taps = jnp.concatenate([taps_ref[k * WIDE : (k + 1) * WIDE, :] for k in range(3)], axis=1)
            gh = cols_dot(side, taps)
            add(half, TAPS_AT, rows_dot(h, side))
            gn = jnp.where(h > 0, gh, 0.0)
            s = lax.rsqrt(mean(x * x) + EPS)
            normed = x * s
            add(half, GAINS_AT, jnp.sum(gn * normed, axis=0, keepdims=True))
            w = gn * gain
            return g + s * (w - normed * mean(w * normed))

        h2 = h2_ref[pl.ds(t0 + LEAD, CHUNK), :]
        gx1 = block(gx2_ref[here, :], x1_ref[here, :], h2, gc2_ref, 1, taps2_ref, gain2_ref[...], 2 * STEP)
        low = gx1.astype(BF)
        a = a1_ref[here, :]
        add(0, OUT_AT, rows_dot(a, low))
        gact = cols_dot(low, out1_ref[...])
        gc1_ref[here, :] = jnp.where(a > 0, gact, 0.0).astype(BF)
        h1 = h1_ref[pl.ds(t0 + LEAD, CHUNK), :]
        gx0 = block(gx1, x0_ref[here, :].astype(F32), h1, gc1_ref, 0, taps1_ref, gain1_ref[...], STEP)
        add(0, 0, rows_dot(hot_ref[here, :], gx0.astype(BF)))
        return carry

    lax.fori_loop(0, n, back, 0)

    core, x = lax.axis_index("core"), lax.axis_index(X)
    for k in range(4):
        at = pl.ds(pl.multiple_of(lax.rem(x + k, 4) * part, part), part)
        keep_refs[k][...] = acc_ref[core, at, :]
        send_refs[k][...] = acc_ref[1 - core, at, :]


def compute(both, weights, loss_scale, peers):
    rows = both.shape[0] * STEP
    part = peers * PART
    vmem, hbm = pl.BlockSpec(memory_space=pltpu.VMEM), pl.BlockSpec(memory_space=pltpu.HBM)
    shapes = [(WIDE, BF), (2 * WIDE, BF), (WIDE, F32)]
    tall = lambda wide, dtype, extra=0: pltpu.VMEM((rows + extra, wide), dtype)
    return pl.pallas_call(
        functools.partial(kernel, peers, loss_scale),
        out_shape=[jax.ShapeDtypeStruct((peers, LANES), BF)] + [jax.ShapeDtypeStruct((part, LANES), F32)] * 8,
        in_specs=[vmem] + [hbm] * len(weights),
        out_specs=[vmem] * 9,
        scratch_shapes=[pltpu.VMEM(w.shape, w.dtype) for w in weights]
        + [
            pltpu.SemaphoreType.DMA((len(weights),)),
            pltpu.VMEM((rows // STEP, STEP), jnp.int32),
            pltpu.VMEM((rows // STEP, STEP), jnp.int32),
            tall(WIDE, BF),
            tall(WIDE, BF),
            tall(WIDE, BF, LEAD),
            tall(2 * WIDE, BF),
            tall(WIDE, F32),
            tall(WIDE, BF, LEAD),
            tall(2 * WIDE, BF),
            tall(WIDE, F32),
            tall(2 * WIDE, BF, LEAD),
            tall(2 * WIDE, BF, LEAD),
            pltpu.VMEM((rows // STEP, STEP), F32),
            pltpu.VMEM((2, 4 * part, LANES), F32),
        ],
        compiler_params=pltpu.CompilerParams(vmem_limit_bytes=57 * 2**20),
    )(both, *weights)


def swap(array, axis, mask):
    count = lax.axis_size(axis)
    return lax.ppermute(array, axis, [(i, i ^ mask) for i in range(count)])


def shift(array, axis, by):
    count = lax.axis_size(axis)
    return lax.ppermute(array, axis, [(i, (i + by) % count) for i in range(count)])


def reduce_all(keep, send, loss):
    parts = [mine + swap(other, "core", 1) for mine, other in zip(keep, send)]
    total = parts[0]
    for k in range(1, 4):
        total = total + shift(parts[k].astype(BF), X, k).astype(F32)
    rest = ("y", "z")
    peers = lax.axis_size(rest)
    message = total.astype(BF).reshape(peers, PART, LANES)
    message = jnp.concatenate([message, jnp.broadcast_to(loss[:, None], (peers, 8, LANES))], axis=1)
    got = lax.all_to_all(message, rest, 0, 0, tiled=True)
    loss = got[:, PART]
    summed = jnp.sum(got[:, :PART].astype(F32), axis=0).astype(BF)
    whole = jnp.broadcast_to(summed[None], (peers, PART, LANES))
    whole = lax.all_to_all(whole, rest, 0, 0, tiled=True).reshape(-1, LANES)
    whole, there = lax.optimization_barrier((whole, swap(loss, "x_lo", 1)))
    mine = [whole] + [shift(whole, X, k) for k in range(1, 4)]
    return mine, [swap(piece, "core", 1) for piece in mine], loss, there


def spread_kernel(*refs):
    mine, others = refs[:4], refs[4:8]
    loss_mine, loss_other = refs[8:10]
    loss_ref, embed, gain1, taps1, out1, gain2, taps2, out2, gainf, head = refs[10:20]
    big, lines = refs[20:]
    core, x, x_lo = lax.axis_index("core"), lax.axis_index(X), lax.axis_index("x_lo")
    part = mine[0].shape[0]
    for k in range(4):
        at = pl.ds(pl.multiple_of(lax.rem(x + 4 - k, 4) * part, part), part)
        big[core, at, :] = mine[k][...]
        big[1 - core, at, :] = others[k][...]

    def write(half, square, taps, out_w, gains):
        def put(target, at, height, count):
            for b in range(count):
                start = at + b * height
                target[:, b * LANES : (b + 1) * LANES] = big[half, start : start + height, :].astype(F32)

        put(square, 0, 256, 2)
        for k in range(3):
            put(taps.at[k], TAPS_AT + 1024 * k, 256, 4)
        put(out_w, OUT_AT, 512, 2)
        tail = big[half, GAINS_AT : GAINS_AT + 16, :].astype(F32)
        for i, gain in enumerate(gains):
            gain[:, :LANES] = tail[2 * i : 2 * i + 1]
            gain[:, LANES:] = tail[2 * i + 1 : 2 * i + 2]

    write(0, embed, taps1, out1, [gain1])
    write(1, head, taps2, out2, [gain2, gainf])

    def joined(ref):
        block = ref[...].astype(F32)
        first = block[:, :STEP] + block[:, STEP : 2 * STEP]
        second = block[:, 2 * STEP : 3 * STEP] + block[:, 3 * STEP :]
        return jnp.where(x_lo == 0, first, second)

    here, there = joined(loss_mine), joined(loss_other)
    half = here.shape[0]
    lines[:half, :] = jnp.where(x_lo == 0, here, there)
    lines[half:, :] = jnp.where(x_lo == 0, there, here)
    for b in range(4):
        loss_ref[:, b * STEP : (b + 1) * STEP] = lines[pl.ds(b, half // 2, stride=4), :]


def spread(mine, others, loss_mine, loss_other):
    vmem = pl.BlockSpec(memory_space=pltpu.VMEM)
    part = mine[0].shape[0]
    peers = loss_mine.shape[0]
    square, taps, out_w, gain = (256, 256), (3, 256, 512), (512, 256), (1, 256)
    shapes = [(peers // 2, LANES), square, gain, taps, out_w, gain, taps, out_w, gain, square]
    return pl.pallas_call(
        spread_kernel,
        out_shape=[jax.ShapeDtypeStruct(s, F32) for s in shapes],
        in_specs=[vmem] * 10,
        out_specs=[vmem] * len(shapes),
        scratch_shapes=[pltpu.VMEM((2, 4 * part, LANES), BF), pltpu.VMEM((2 * peers, STEP), F32)],
        compiler_params=pltpu.CompilerParams(vmem_limit_bytes=32 * 2**20),
    )(*mine, *others, loss_mine, loss_other)


def local(tokens, targets, embed, gain1, taps1, out1, gain2, taps2, out2, gainf, head):
    ctx = ("x_lo", "y", "z")
    count = tokens.shape[1]
    shards = lax.axis_size(ctx)
    loss_scale = float(count * shards * lax.axis_size(("x_hi", "core"))) ** (-0.5)
    lines = jnp.stack([tokens.reshape(-1, LANES), targets.reshape(-1, LANES)], axis=1)
    both = jnp.broadcast_to(lines[:, None], (lines.shape[0], 4, 2, LANES)).reshape(shards, 2, LANES)
    both = lax.all_to_all(both, ctx, 0, 0, tiled=True)
    weights = (
        embed,
        gain1[None],
        taps1.reshape(-1, 512),
        out1,
        gain2[None],
        taps2.reshape(-1, 512),
        out2,
        gainf[None],
        head,
    )
    outs = compute(both, weights, loss_scale, shards // 2)
    mine, others, loss_mine, loss_other = reduce_all(outs[1:5], outs[5:9], outs[0])
    loss, *grads = spread(mine, others, loss_mine, loss_other)
    for i in (1, 4, 7):
        grads[i] = grads[i][0]
    return (loss.reshape(1, count), *grads)


def solution(mesh):
    fine = Mesh(mesh.devices.reshape(2, 2, 2, 4, 8), ("x_hi", "core", "x_lo", "y", "z"))
    data = P(("x_hi", "core"), ("x_lo", "y", "z"))
    in_specs = (data, data, P(), P(), P(), P(), P(), P(), P(), P(), P())
    out_specs = (data, P(), P(), P(), P(), P(), P(), P(), P(), P())
    return jax.shard_map(local, mesh=fine, in_specs=in_specs, out_specs=out_specs, check_vma=False)
```

```python
import functools

import jax
import jax.numpy as jnp
from jax import lax
from jax.experimental import pallas as pl
from jax.experimental.pallas import tpu as pltpu
from jax.sharding import Mesh, PartitionSpec as P

EPS = 1e-05
BF = jnp.bfloat16
F32 = jnp.float32
WIDE = 256
LANES = 128
LEAD = 128
CHUNK = 1024
STEP = 32
PART = 40
TAPS_AT, OUT_AT, GAINS_AT = 512, 3584, 4608
X = ("x_hi", "x_lo")


def rows_dot(left, right):
    return lax.dot_general(left, right, (((0,), (0,)), ((), ())), preferred_element_type=F32)


def by_halves(product, left, right, wide):
    if wide > WIDE:
        return product(left, right)
    half = left.shape[0] // 2
    return jnp.concatenate([product(left[:half], right), product(left[half:], right)], axis=0)


def cols_dot(left, right):
    product = lambda a, b: lax.dot_general(a, b, (((1,), (1,)), ((), ())), preferred_element_type=F32)
    return by_halves(product, left, right, right.shape[0])


def dot(left, right):
    product = lambda a, b: jnp.dot(a, b, preferred_element_type=F32)
    return by_halves(product, left, right, right.shape[1])


def mean(values):
    return jnp.sum(values, axis=-1, keepdims=True) * (1.0 / WIDE)


def kernel(
    peers,
    loss_scale,
    both_ref,
    embed_hbm,
    gain1_hbm,
    taps1_hbm,
    out1_hbm,
    gain2_hbm,
    taps2_hbm,
    out2_hbm,
    gainf_hbm,
    head_hbm,
    loss_ref,
    *rest,
):
    part = peers * PART
    keep_refs, send_refs = rest[:4], rest[4:8]
    (embed_ref, gain1_ref, taps1_ref, out1_ref, gain2_ref, taps2_ref, out2_ref, gainf_ref, head_ref) = rest[8:17]
    (sems, tok_ref, targ_ref, hot_ref, x0_ref, h1_ref, a1_ref, x1_ref, h2_ref, a2_ref, gx2_ref, gc2_ref, gc1_ref) = rest[17:30]
    losses_ref, acc0_ref, acc1_ref, out_sems = rest[30:]
    accs = (acc0_ref, acc1_ref)
    sources = (embed_hbm, gain1_hbm, taps1_hbm, out1_hbm, gain2_hbm, taps2_hbm, out2_hbm, gainf_hbm, head_hbm)
    copies = [pltpu.make_async_copy(src, dst, sems.at[i]) for i, (src, dst) in enumerate(zip(sources, rest[8:17]))]
    for copy in copies:
        copy.start()
    rows = x0_ref.shape[0]
    n = rows // CHUNK
    shards = CHUNK // STEP
    zeros = jnp.zeros((LEAD, WIDE), BF)
    h1_ref[0:LEAD, :] = zeros
    h2_ref[0:LEAD, :] = zeros
    gc1_ref[rows : rows + LEAD, :] = jnp.zeros((LEAD, 2 * WIDE), BF)
    gc2_ref[rows : rows + LEAD, :] = jnp.zeros((LEAD, 2 * WIDE), BF)
    acc0_ref[...] = jnp.zeros_like(acc0_ref)
    acc1_ref[...] = jnp.zeros_like(acc1_ref)
    quarter = lax.rem(lax.axis_index("z"), 4)

    def mine(block):
        pieces = [block[:, STEP * p : STEP * (p + 1)] for p in range(4)]
        low = jnp.where(quarter == 0, pieces[0], pieces[1])
        high = jnp.where(quarter == 2, pieces[2], pieces[3])
        return jnp.where(quarter < 2, low, high)

    tok_ref[...] = mine(both_ref[:, 0, :])
    targ_ref[...] = mine(both_ref[:, 1, :])
    letters = lax.broadcasted_iota(jnp.int32, (CHUNK, WIDE), 1)
    diagonal = lax.rem(lax.broadcasted_iota(jnp.int32, (CHUNK, STEP), 0), STEP) == lax.broadcasted_iota(
        jnp.int32, (CHUNK, STEP), 1
    )

    def column(ref, i):
        block = ref[pl.ds(pl.multiple_of(i * shards, shards), shards), :]
        tall = jnp.broadcast_to(block[:, None, :], (shards, STEP, STEP)).reshape(CHUNK, STEP)
        return jnp.sum(jnp.where(diagonal, tall, 0), axis=1, keepdims=True)

    def add(half, at, value):
        height = value.shape[0]
        for b in range(value.shape[1] // LANES):
            start = at + b * height
            accs[half][start : start + height, :] += value[:, b * LANES : (b + 1) * LANES]

    for copy in copies:
        copy.wait()

    def forward(i, carry):
        t0 = pl.multiple_of(i * CHUNK, CHUNK)
        here = pl.ds(t0, CHUNK)
        onehot = (column(tok_ref, i) == letters).astype(F32).astype(BF)
        hot_ref[here, :] = onehot
        x0 = dot(onehot, embed_ref[...])
        x0_ref[here, :] = x0.astype(BF)

        def layer(x, gain_ref, taps_ref, out_ref, h_ref, a_ref, dist):
            s = lax.rsqrt(mean(x * x) + EPS)
            h = jnp.maximum(x * s * gain_ref[...], 0.0).astype(BF)
            h_ref[pl.ds(t0 + LEAD, CHUNK), :] = h
            near = h_ref[pl.ds(t0 + LEAD - dist, CHUNK), :]
            far = h_ref[pl.ds(t0 + LEAD - 2 * dist, CHUNK), :]
            a = jnp.maximum(dot(jnp.concatenate([h, near, far], axis=1), taps_ref[...]), 0.0).astype(BF)
            a_ref[here, :] = a
            return x + dot(a, out_ref[...]), a

        x1, _ = layer(x0, gain1_ref, taps1_ref, out1_ref, h1_ref, a1_ref, STEP)
        x1_ref[here, :] = x1
        x2, a = layer(x1, gain2_ref, taps2_ref, out2_ref, h2_ref, a2_ref, 2 * STEP)
        s = lax.rsqrt(mean(x2 * x2) + EPS)
        normed = x2 * s
        final = (normed * gainf_ref[...]).astype(BF)
        logits = dot(final, head_ref[...])
        highest = jnp.max(logits, axis=1, keepdims=True)
        e = jnp.exp(logits - highest)
        total = jnp.sum(e, axis=1, keepdims=True)
        wanted = (column(targ_ref, i) == letters).astype(F32)
        loss = highest + jnp.log(total) - jnp.sum(logits * wanted, axis=1, keepdims=True)
        spread = jnp.where(diagonal, loss, 0.0).reshape(shards, STEP, STEP)
        losses_ref[pl.ds(pl.multiple_of(i * shards, shards), shards), :] = jnp.sum(spread, axis=1)
        gl = ((e * (1.0 / total) - wanted) * loss_scale).astype(BF)
        add(1, 0, rows_dot(final, gl))
        gfin = cols_dot(gl, head_ref[...])
        add(1, GAINS_AT + 2, jnp.sum(gfin * normed, axis=0, keepdims=True))
        w = gfin * gainf_ref[...]
        gx2 = s * (w - normed * mean(w * normed))
        gx2_ref[here, :] = gx2
        low = gx2.astype(BF)
        add(1, OUT_AT, rows_dot(a, low))
        gact = cols_dot(low, out2_ref[...])
        gc2_ref[here, :] = jnp.where(a > 0, gact, 0.0).astype(BF)
        return carry

    lax.fori_loop(0, n, forward, 0)

    losses = losses_ref[...]
    high = losses.astype(BF).astype(F32)
    low = losses - high
    half = peers
    loss_ref[...] = jnp.concatenate([high[:half], low[:half], high[half:], low[half:]], axis=1).astype(BF)

    core, x = lax.axis_index("core"), lax.axis_index(X)

    def leave(half, begin):
        for kept in (True, False):
            targets = keep_refs if kept else send_refs

            @pl.when((core == half) == kept)
            def _():
                for k in range(4):
                    at = pl.ds(pl.multiple_of(lax.rem(x + k, 4) * part, part), part)
                    copy = pltpu.make_async_copy(accs[half].at[at, :], targets[k], out_sems.at[half, k])
                    if begin:
                        copy.start()
                    else:
                        copy.wait()

    def back(i, carry):
        j = n - 1 - i
        t0 = pl.multiple_of(j * CHUNK, CHUNK)
        here = pl.ds(t0, CHUNK)

        def block(g, x, h, gc_ref, half, taps_ref, gain, dist):
            gcs = [gc_ref[pl.ds(t0 + k * dist, CHUNK), :] for k in range(3)]
            side = jnp.concatenate(gcs, axis=1)
            taps = jnp.concatenate([taps_ref[k * WIDE : (k + 1) * WIDE, :] for k in range(3)], axis=1)
            gh = cols_dot(side, taps)
            add(half, TAPS_AT, rows_dot(h, side))
            gn = jnp.where(h > 0, gh, 0.0)
            s = lax.rsqrt(mean(x * x) + EPS)
            normed = x * s
            add(half, GAINS_AT, jnp.sum(gn * normed, axis=0, keepdims=True))
            w = gn * gain
            return g + s * (w - normed * mean(w * normed))

        h2 = h2_ref[pl.ds(t0 + LEAD, CHUNK), :]
        gx1 = block(gx2_ref[here, :], x1_ref[here, :], h2, gc2_ref, 1, taps2_ref, gain2_ref[...], 2 * STEP)

        @pl.when(i == n - 1)
        def _():
            leave(1, True)

        low = gx1.astype(BF)
        a = a1_ref[here, :]
        add(0, OUT_AT, rows_dot(a, low))
        gact = cols_dot(low, out1_ref[...])
        gc1_ref[here, :] = jnp.where(a > 0, gact, 0.0).astype(BF)
        h1 = h1_ref[pl.ds(t0 + LEAD, CHUNK), :]
        gx0 = block(gx1, x0_ref[here, :].astype(F32), h1, gc1_ref, 0, taps1_ref, gain1_ref[...], STEP)
        add(0, 0, rows_dot(hot_ref[here, :], gx0.astype(BF)))
        return carry

    lax.fori_loop(0, n, back, 0)

    leave(0, True)
    leave(1, False)
    leave(0, False)


def compute(both, weights, loss_scale, peers):
    rows = both.shape[0] * STEP
    part = peers * PART
    vmem, hbm = pl.BlockSpec(memory_space=pltpu.VMEM), pl.BlockSpec(memory_space=pltpu.HBM)
    shapes = [(WIDE, BF), (2 * WIDE, BF), (WIDE, F32)]
    tall = lambda wide, dtype, extra=0: pltpu.VMEM((rows + extra, wide), dtype)
    return pl.pallas_call(
        functools.partial(kernel, peers, loss_scale),
        out_shape=[jax.ShapeDtypeStruct((peers, LANES), BF)] + [jax.ShapeDtypeStruct((part, LANES), F32)] * 8,
        in_specs=[vmem] + [hbm] * len(weights),
        out_specs=[vmem] + [hbm] * 8,
        scratch_shapes=[pltpu.VMEM(w.shape, w.dtype) for w in weights]
        + [
            pltpu.SemaphoreType.DMA((len(weights),)),
            pltpu.VMEM((rows // STEP, STEP), jnp.int32),
            pltpu.VMEM((rows // STEP, STEP), jnp.int32),
            tall(WIDE, BF),
            tall(WIDE, BF),
            tall(WIDE, BF, LEAD),
            tall(2 * WIDE, BF),
            tall(WIDE, F32),
            tall(WIDE, BF, LEAD),
            tall(2 * WIDE, BF),
            tall(WIDE, F32),
            tall(2 * WIDE, BF, LEAD),
            tall(2 * WIDE, BF, LEAD),
            pltpu.VMEM((rows // STEP, STEP), F32),
            pltpu.VMEM((4 * part, LANES), F32),
            pltpu.VMEM((4 * part, LANES), F32),
            pltpu.SemaphoreType.DMA((2, 4)),
        ],
        compiler_params=pltpu.CompilerParams(vmem_limit_bytes=57 * 2**20),
    )(both, *weights)


def swap(array, axis, mask):
    count = lax.axis_size(axis)
    return lax.ppermute(array, axis, [(i, i ^ mask) for i in range(count)])


def shift(array, axis, by):
    count = lax.axis_size(axis)
    return lax.ppermute(array, axis, [(i, (i + by) % count) for i in range(count)])


def reduce_all(keep, send, loss):
    parts = [mine + swap(other, "core", 1) for mine, other in zip(keep, send)]
    total = parts[0]
    for k in range(1, 4):
        total = total + shift(parts[k].astype(BF), X, k).astype(F32)
    rest = ("y", "z")
    peers = lax.axis_size(rest)
    message = total.astype(BF).reshape(peers, PART, LANES)
    message = jnp.concatenate([message, jnp.broadcast_to(loss[:, None], (peers, 8, LANES))], axis=1)
    got = lax.all_to_all(message, rest, 0, 0, tiled=True)
    loss = got[:, PART]
    summed = jnp.sum(got[:, :PART].astype(F32), axis=0).astype(BF)
    whole = jnp.broadcast_to(summed[None], (peers, PART, LANES))
    whole = lax.all_to_all(whole, rest, 0, 0, tiled=True).reshape(-1, LANES)
    whole, there = lax.optimization_barrier((whole, swap(loss, "x_lo", 1)))
    mine = [whole] + [shift(whole, X, k) for k in range(1, 4)]
    return mine, [swap(piece, "core", 1) for piece in mine], loss, there


def spread_kernel(*refs):
    mine, others = refs[:4], refs[4:8]
    loss_mine, loss_other = refs[8:10]
    loss_ref, embed, gain1, taps1, out1, gain2, taps2, out2, gainf, head = refs[10:20]
    big, lines = refs[20:]
    core, x, x_lo = lax.axis_index("core"), lax.axis_index(X), lax.axis_index("x_lo")
    part = mine[0].shape[0]
    for k in range(4):
        at = pl.ds(pl.multiple_of(lax.rem(x + 4 - k, 4) * part, part), part)
        big[core, at, :] = mine[k][...]
        big[1 - core, at, :] = others[k][...]

    def write(half, square, taps, out_w, gains):
        def put(target, at, height, count):
            for b in range(count):
                start = at + b * height
                target[:, b * LANES : (b + 1) * LANES] = big[half, start : start + height, :].astype(F32)

        put(square, 0, 256, 2)
        for k in range(3):
            put(taps.at[k], TAPS_AT + 1024 * k, 256, 4)
        put(out_w, OUT_AT, 512, 2)
        tail = big[half, GAINS_AT : GAINS_AT + 16, :].astype(F32)
        for i, gain in enumerate(gains):
            gain[:, :LANES] = tail[2 * i : 2 * i + 1]
            gain[:, LANES:] = tail[2 * i + 1 : 2 * i + 2]

    write(0, embed, taps1, out1, [gain1])
    write(1, head, taps2, out2, [gain2, gainf])

    def joined(ref):
        block = ref[...].astype(F32)
        first = block[:, :STEP] + block[:, STEP : 2 * STEP]
        second = block[:, 2 * STEP : 3 * STEP] + block[:, 3 * STEP :]
        return jnp.where(x_lo == 0, first, second)

    here, there = joined(loss_mine), joined(loss_other)
    half = here.shape[0]
    lines[:half, :] = jnp.where(x_lo == 0, here, there)
    lines[half:, :] = jnp.where(x_lo == 0, there, here)
    for b in range(4):
        loss_ref[:, b * STEP : (b + 1) * STEP] = lines[pl.ds(b, half // 2, stride=4), :]


def spread(mine, others, loss_mine, loss_other):
    vmem = pl.BlockSpec(memory_space=pltpu.VMEM)
    part = mine[0].shape[0]
    peers = loss_mine.shape[0]
    square, taps, out_w, gain = (256, 256), (3, 256, 512), (512, 256), (1, 256)
    shapes = [(peers // 2, LANES), square, gain, taps, out_w, gain, taps, out_w, gain, square]
    return pl.pallas_call(
        spread_kernel,
        out_shape=[jax.ShapeDtypeStruct(s, F32) for s in shapes],
        in_specs=[vmem] * 10,
        out_specs=[vmem] * len(shapes),
        scratch_shapes=[pltpu.VMEM((2, 4 * part, LANES), BF), pltpu.VMEM((2 * peers, STEP), F32)],
        compiler_params=pltpu.CompilerParams(vmem_limit_bytes=32 * 2**20),
    )(*mine, *others, loss_mine, loss_other)


def local(tokens, targets, embed, gain1, taps1, out1, gain2, taps2, out2, gainf, head):
    ctx = ("x_lo", "y", "z")
    count = tokens.shape[1]
    shards = lax.axis_size(ctx)
    loss_scale = float(count * shards * lax.axis_size(("x_hi", "core"))) ** (-0.5)
    lines = jnp.stack([tokens.reshape(-1, LANES), targets.reshape(-1, LANES)], axis=1)
    both = jnp.broadcast_to(lines[:, None], (lines.shape[0], 4, 2, LANES)).reshape(shards, 2, LANES)
    both = lax.all_to_all(both, ctx, 0, 0, tiled=True)
    weights = (
        embed,
        gain1[None],
        taps1.reshape(-1, 512),
        out1,
        gain2[None],
        taps2.reshape(-1, 512),
        out2,
        gainf[None],
        head,
    )
    outs = compute(both, weights, loss_scale, shards // 2)
    mine, others, loss_mine, loss_other = reduce_all(outs[1:5], outs[5:9], outs[0])
    loss, *grads = spread(mine, others, loss_mine, loss_other)
    for i in (1, 4, 7):
        grads[i] = grads[i][0]
    return (loss.reshape(1, count), *grads)


def solution(mesh):
    fine = Mesh(mesh.devices.reshape(2, 2, 2, 4, 8), ("x_hi", "core", "x_lo", "y", "z"))
    data = P(("x_hi", "core"), ("x_lo", "y", "z"))
    in_specs = (data, data, P(), P(), P(), P(), P(), P(), P(), P(), P())
    out_specs = (data, P(), P(), P(), P(), P(), P(), P(), P(), P())
    return jax.shard_map(local, mesh=fine, in_specs=in_specs, out_specs=out_specs, check_vma=False)
```

```python
import functools

import jax
import jax.numpy as jnp
from jax import lax
from jax.experimental import pallas as pl
from jax.experimental.pallas import tpu as pltpu
from jax.sharding import Mesh, PartitionSpec as P

EPS = 1e-05
BF = jnp.bfloat16
F32 = jnp.float32
WIDE = 256
LANES = 128
LEAD = 128
CHUNK = 1024
BACK = 2048
STEP = 32
PART = 40
TAPS_AT, OUT_AT, GAINS_AT = 512, 3584, 4608
X = ("x_hi", "x_lo")


def rows_dot(left, right):
    return lax.dot_general(left, right, (((0,), (0,)), ((), ())), preferred_element_type=F32)


def by_halves(product, left, right, wide):
    if wide > WIDE:
        return product(left, right)
    half = left.shape[0] // 2
    return jnp.concatenate([product(left[:half], right), product(left[half:], right)], axis=0)


def cols_dot(left, right):
    product = lambda a, b: lax.dot_general(a, b, (((1,), (1,)), ((), ())), preferred_element_type=F32)
    return by_halves(product, left, right, right.shape[0])


def dot(left, right):
    product = lambda a, b: jnp.dot(a, b, preferred_element_type=F32)
    return by_halves(product, left, right, right.shape[1])


def mean(values):
    return jnp.sum(values, axis=-1, keepdims=True) * (1.0 / WIDE)


def kernel(
    peers,
    loss_scale,
    both_ref,
    embed_hbm,
    gain1_hbm,
    taps1_hbm,
    out1_hbm,
    gain2_hbm,
    taps2_hbm,
    out2_hbm,
    gainf_hbm,
    head_hbm,
    loss_ref,
    *rest,
):
    part = peers * PART
    keep_refs, send_refs = rest[:4], rest[4:8]
    (embed_ref, gain1_ref, taps1_ref, out1_ref, gain2_ref, taps2_ref, out2_ref, gainf_ref, head_ref) = rest[8:17]
    (sems, tok_ref, targ_ref, hot_ref, x0_ref, h1_ref, a1_ref, x1_ref, h2_ref, a2_ref, gx2_ref, gc2_ref, gc1_ref) = rest[17:30]
    losses_ref, acc0_ref, acc1_ref, out_sems = rest[30:]
    accs = (acc0_ref, acc1_ref)
    sources = (embed_hbm, gain1_hbm, taps1_hbm, out1_hbm, gain2_hbm, taps2_hbm, out2_hbm, gainf_hbm, head_hbm)
    copies = [pltpu.make_async_copy(src, dst, sems.at[i]) for i, (src, dst) in enumerate(zip(sources, rest[8:17]))]
    for copy in copies:
        copy.start()
    rows = x0_ref.shape[0]
    n = rows // CHUNK
    shards = CHUNK // STEP
    zeros = jnp.zeros((LEAD, WIDE), BF)
    h1_ref[0:LEAD, :] = zeros
    h2_ref[0:LEAD, :] = zeros
    gc1_ref[rows : rows + LEAD, :] = jnp.zeros((LEAD, 2 * WIDE), BF)
    gc2_ref[rows : rows + LEAD, :] = jnp.zeros((LEAD, 2 * WIDE), BF)
    acc0_ref[...] = jnp.zeros_like(acc0_ref)
    acc1_ref[...] = jnp.zeros_like(acc1_ref)
    quarter = lax.rem(lax.axis_index("z"), 4)

    def mine(block):
        pieces = [block[:, STEP * p : STEP * (p + 1)] for p in range(4)]
        low = jnp.where(quarter == 0, pieces[0], pieces[1])
        high = jnp.where(quarter == 2, pieces[2], pieces[3])
        return jnp.where(quarter < 2, low, high)

    tok_ref[...] = mine(both_ref[:, 0, :])
    targ_ref[...] = mine(both_ref[:, 1, :])
    letters = lax.broadcasted_iota(jnp.int32, (CHUNK, WIDE), 1)
    diagonal = lax.rem(lax.broadcasted_iota(jnp.int32, (CHUNK, STEP), 0), STEP) == lax.broadcasted_iota(
        jnp.int32, (CHUNK, STEP), 1
    )

    def column(ref, i):
        block = ref[pl.ds(pl.multiple_of(i * shards, shards), shards), :]
        tall = jnp.broadcast_to(block[:, None, :], (shards, STEP, STEP)).reshape(CHUNK, STEP)
        return jnp.sum(jnp.where(diagonal, tall, 0), axis=1, keepdims=True)

    def add(half, at, value):
        height = value.shape[0]
        for b in range(value.shape[1] // LANES):
            start = at + b * height
            accs[half][start : start + height, :] += value[:, b * LANES : (b + 1) * LANES]

    for copy in copies:
        copy.wait()

    def forward(i, carry):
        t0 = pl.multiple_of(i * CHUNK, CHUNK)
        here = pl.ds(t0, CHUNK)
        onehot = (column(tok_ref, i) == letters).astype(F32).astype(BF)
        hot_ref[here, :] = onehot
        x0 = dot(onehot, embed_ref[...])
        x0_ref[here, :] = x0.astype(BF)

        def layer(x, gain_ref, taps_ref, out_ref, h_ref, a_ref, dist):
            s = lax.rsqrt(mean(x * x) + EPS)
            h = jnp.maximum(x * s * gain_ref[...], 0.0).astype(BF)
            h_ref[pl.ds(t0 + LEAD, CHUNK), :] = h
            near = h_ref[pl.ds(t0 + LEAD - dist, CHUNK), :]
            far = h_ref[pl.ds(t0 + LEAD - 2 * dist, CHUNK), :]
            a = jnp.maximum(dot(jnp.concatenate([h, near, far], axis=1), taps_ref[...]), 0.0).astype(BF)
            a_ref[here, :] = a
            return x + dot(a, out_ref[...]), a

        x1, _ = layer(x0, gain1_ref, taps1_ref, out1_ref, h1_ref, a1_ref, STEP)
        x1_ref[here, :] = x1
        x2, a = layer(x1, gain2_ref, taps2_ref, out2_ref, h2_ref, a2_ref, 2 * STEP)
        s = lax.rsqrt(mean(x2 * x2) + EPS)
        normed = x2 * s
        final = (normed * gainf_ref[...]).astype(BF)
        logits = dot(final, head_ref[...])
        highest = jnp.max(logits, axis=1, keepdims=True)
        e = jnp.exp(logits - highest)
        total = jnp.sum(e, axis=1, keepdims=True)
        wanted = (column(targ_ref, i) == letters).astype(F32)
        loss = highest + jnp.log(total) - jnp.sum(logits * wanted, axis=1, keepdims=True)
        spread = jnp.where(diagonal, loss, 0.0).reshape(shards, STEP, STEP)
        losses_ref[pl.ds(pl.multiple_of(i * shards, shards), shards), :] = jnp.sum(spread, axis=1)
        gl = ((e * (1.0 / total) - wanted) * loss_scale).astype(BF)
        add(1, 0, rows_dot(final, gl))
        gfin = cols_dot(gl, head_ref[...])
        add(1, GAINS_AT + 2, jnp.sum(gfin * normed, axis=0, keepdims=True))
        w = gfin * gainf_ref[...]
        gx2 = s * (w - normed * mean(w * normed))
        gx2_ref[here, :] = gx2
        low = gx2.astype(BF)
        add(1, OUT_AT, rows_dot(a, low))
        gact = cols_dot(low, out2_ref[...])
        gc2_ref[here, :] = jnp.where(a > 0, gact, 0.0).astype(BF)
        return carry

    lax.fori_loop(0, n, forward, 0)

    losses = losses_ref[...]
    high = losses.astype(BF).astype(F32)
    low = losses - high
    half = peers
    loss_ref[...] = jnp.concatenate([high[:half], low[:half], high[half:], low[half:]], axis=1).astype(BF)

    core, x = lax.axis_index("core"), lax.axis_index(X)

    def leave(half, begin):
        for kept in (True, False):
            targets = keep_refs if kept else send_refs

            @pl.when((core == half) == kept)
            def _():
                for k in range(4):
                    at = pl.ds(pl.multiple_of(lax.rem(x + k, 4) * part, part), part)
                    copy = pltpu.make_async_copy(accs[half].at[at, :], targets[k], out_sems.at[half, k])
                    if begin:
                        copy.start()
                    else:
                        copy.wait()

    def back(i, carry):
        j = rows // BACK - 1 - i
        t0 = pl.multiple_of(j * BACK, BACK)
        here = pl.ds(t0, BACK)

        def block(g, x, h, gc_ref, half, taps_ref, gain, dist):
            gcs = [gc_ref[pl.ds(t0 + k * dist, BACK), :] for k in range(3)]
            side = jnp.concatenate(gcs, axis=1)
            taps = jnp.concatenate([taps_ref[k * WIDE : (k + 1) * WIDE, :] for k in range(3)], axis=1)
            gh = cols_dot(side, taps)
            add(half, TAPS_AT, rows_dot(h, side))
            gn = jnp.where(h > 0, gh, 0.0)
            s = lax.rsqrt(mean(x * x) + EPS)
            normed = x * s
            add(half, GAINS_AT, jnp.sum(gn * normed, axis=0, keepdims=True))
            w = gn * gain
            return g + s * (w - normed * mean(w * normed))

        h2 = h2_ref[pl.ds(t0 + LEAD, BACK), :]
        gx1 = block(gx2_ref[here, :], x1_ref[here, :], h2, gc2_ref, 1, taps2_ref, gain2_ref[...], 2 * STEP)

        @pl.when(i == rows // BACK - 1)
        def _():
            leave(1, True)

        low = gx1.astype(BF)
        a = a1_ref[here, :]
        add(0, OUT_AT, rows_dot(a, low))
        gact = cols_dot(low, out1_ref[...])
        gc1_ref[here, :] = jnp.where(a > 0, gact, 0.0).astype(BF)
        h1 = h1_ref[pl.ds(t0 + LEAD, BACK), :]
        gx0 = block(gx1, x0_ref[here, :].astype(F32), h1, gc1_ref, 0, taps1_ref, gain1_ref[...], STEP)
        add(0, 0, rows_dot(hot_ref[here, :], gx0.astype(BF)))
        return carry

    lax.fori_loop(0, rows // BACK, back, 0)

    leave(0, True)
    leave(1, False)
    leave(0, False)


def compute(both, weights, loss_scale, peers):
    rows = both.shape[0] * STEP
    part = peers * PART
    vmem, hbm = pl.BlockSpec(memory_space=pltpu.VMEM), pl.BlockSpec(memory_space=pltpu.HBM)
    shapes = [(WIDE, BF), (2 * WIDE, BF), (WIDE, F32)]
    tall = lambda wide, dtype, extra=0: pltpu.VMEM((rows + extra, wide), dtype)
    return pl.pallas_call(
        functools.partial(kernel, peers, loss_scale),
        out_shape=[jax.ShapeDtypeStruct((peers, LANES), BF)] + [jax.ShapeDtypeStruct((part, LANES), F32)] * 8,
        in_specs=[vmem] + [hbm] * len(weights),
        out_specs=[vmem] + [hbm] * 8,
        scratch_shapes=[pltpu.VMEM(w.shape, w.dtype) for w in weights]
        + [
            pltpu.SemaphoreType.DMA((len(weights),)),
            pltpu.VMEM((rows // STEP, STEP), jnp.int32),
            pltpu.VMEM((rows // STEP, STEP), jnp.int32),
            tall(WIDE, BF),
            tall(WIDE, BF),
            tall(WIDE, BF, LEAD),
            tall(2 * WIDE, BF),
            tall(WIDE, F32),
            tall(WIDE, BF, LEAD),
            tall(2 * WIDE, BF),
            tall(WIDE, F32),
            tall(2 * WIDE, BF, LEAD),
            tall(2 * WIDE, BF, LEAD),
            pltpu.VMEM((rows // STEP, STEP), F32),
            pltpu.VMEM((4 * part, LANES), F32),
            pltpu.VMEM((4 * part, LANES), F32),
            pltpu.SemaphoreType.DMA((2, 4)),
        ],
        compiler_params=pltpu.CompilerParams(vmem_limit_bytes=57 * 2**20),
    )(both, *weights)


def swap(array, axis, mask):
    count = lax.axis_size(axis)
    return lax.ppermute(array, axis, [(i, i ^ mask) for i in range(count)])


def shift(array, axis, by):
    count = lax.axis_size(axis)
    return lax.ppermute(array, axis, [(i, (i + by) % count) for i in range(count)])


def reduce_all(keep, send, loss):
    parts = [mine + swap(other, "core", 1) for mine, other in zip(keep, send)]
    total = parts[0]
    for k in range(1, 4):
        total = total + shift(parts[k].astype(BF), X, k).astype(F32)
    rest = ("y", "z")
    peers = lax.axis_size(rest)
    message = total.astype(BF).reshape(peers, PART, LANES)
    message = jnp.concatenate([message, jnp.broadcast_to(loss[:, None], (peers, 8, LANES))], axis=1)
    got = lax.all_to_all(message, rest, 0, 0, tiled=True)
    loss = got[:, PART]
    summed = jnp.sum(got[:, :PART].astype(F32), axis=0).astype(BF)
    whole = jnp.broadcast_to(summed[None], (peers, PART, LANES))
    whole = lax.all_to_all(whole, rest, 0, 0, tiled=True).reshape(-1, LANES)
    whole, there = lax.optimization_barrier((whole, swap(loss, "x_lo", 1)))
    mine = [whole] + [shift(whole, X, k) for k in range(1, 4)]
    return mine, [swap(piece, "core", 1) for piece in mine], loss, there


def spread_kernel(*refs):
    mine, others = refs[:4], refs[4:8]
    loss_mine, loss_other = refs[8:10]
    loss_ref, embed, gain1, taps1, out1, gain2, taps2, out2, gainf, head = refs[10:20]
    big, lines = refs[20:]
    core, x, x_lo = lax.axis_index("core"), lax.axis_index(X), lax.axis_index("x_lo")
    part = mine[0].shape[0]
    for k in range(4):
        at = pl.ds(pl.multiple_of(lax.rem(x + 4 - k, 4) * part, part), part)
        big[core, at, :] = mine[k][...]
        big[1 - core, at, :] = others[k][...]

    def write(half, square, taps, out_w, gains):
        def put(target, at, height, count):
            for b in range(count):
                start = at + b * height
                target[:, b * LANES : (b + 1) * LANES] = big[half, start : start + height, :].astype(F32)

        put(square, 0, 256, 2)
        for k in range(3):
            put(taps.at[k], TAPS_AT + 1024 * k, 256, 4)
        put(out_w, OUT_AT, 512, 2)
        tail = big[half, GAINS_AT : GAINS_AT + 16, :].astype(F32)
        for i, gain in enumerate(gains):
            gain[:, :LANES] = tail[2 * i : 2 * i + 1]
            gain[:, LANES:] = tail[2 * i + 1 : 2 * i + 2]

    write(0, embed, taps1, out1, [gain1])
    write(1, head, taps2, out2, [gain2, gainf])

    def joined(ref):
        block = ref[...].astype(F32)
        first = block[:, :STEP] + block[:, STEP : 2 * STEP]
        second = block[:, 2 * STEP : 3 * STEP] + block[:, 3 * STEP :]
        return jnp.where(x_lo == 0, first, second)

    here, there = joined(loss_mine), joined(loss_other)
    half = here.shape[0]
    lines[:half, :] = jnp.where(x_lo == 0, here, there)
    lines[half:, :] = jnp.where(x_lo == 0, there, here)
    for b in range(4):
        loss_ref[:, b * STEP : (b + 1) * STEP] = lines[pl.ds(b, half // 2, stride=4), :]


def spread(mine, others, loss_mine, loss_other):
    vmem = pl.BlockSpec(memory_space=pltpu.VMEM)
    part = mine[0].shape[0]
    peers = loss_mine.shape[0]
    square, taps, out_w, gain = (256, 256), (3, 256, 512), (512, 256), (1, 256)
    shapes = [(peers // 2, LANES), square, gain, taps, out_w, gain, taps, out_w, gain, square]
    return pl.pallas_call(
        spread_kernel,
        out_shape=[jax.ShapeDtypeStruct(s, F32) for s in shapes],
        in_specs=[vmem] * 10,
        out_specs=[vmem] * len(shapes),
        scratch_shapes=[pltpu.VMEM((2, 4 * part, LANES), BF), pltpu.VMEM((2 * peers, STEP), F32)],
        compiler_params=pltpu.CompilerParams(vmem_limit_bytes=32 * 2**20),
    )(*mine, *others, loss_mine, loss_other)


def local(tokens, targets, embed, gain1, taps1, out1, gain2, taps2, out2, gainf, head):
    ctx = ("x_lo", "y", "z")
    count = tokens.shape[1]
    shards = lax.axis_size(ctx)
    loss_scale = float(count * shards * lax.axis_size(("x_hi", "core"))) ** (-0.5)
    lines = jnp.stack([tokens.reshape(-1, LANES), targets.reshape(-1, LANES)], axis=1)
    both = jnp.broadcast_to(lines[:, None], (lines.shape[0], 4, 2, LANES)).reshape(shards, 2, LANES)
    both = lax.all_to_all(both, ctx, 0, 0, tiled=True)
    weights = (
        embed,
        gain1[None],
        taps1.reshape(-1, 512),
        out1,
        gain2[None],
        taps2.reshape(-1, 512),
        out2,
        gainf[None],
        head,
    )
    outs = compute(both, weights, loss_scale, shards // 2)
    mine, others, loss_mine, loss_other = reduce_all(outs[1:5], outs[5:9], outs[0])
    loss, *grads = spread(mine, others, loss_mine, loss_other)
    for i in (1, 4, 7):
        grads[i] = grads[i][0]
    return (loss.reshape(1, count), *grads)


def solution(mesh):
    fine = Mesh(mesh.devices.reshape(2, 2, 2, 4, 8), ("x_hi", "core", "x_lo", "y", "z"))
    data = P(("x_hi", "core"), ("x_lo", "y", "z"))
    in_specs = (data, data, P(), P(), P(), P(), P(), P(), P(), P(), P())
    out_specs = (data, P(), P(), P(), P(), P(), P(), P(), P(), P())
    return jax.shard_map(local, mesh=fine, in_specs=in_specs, out_specs=out_specs, check_vma=False)
```
